32 devices in a mesh: slab: 8 (over z, x), img: 4 (over y, core).
Axes of the slice: x: 2, y: 2, z: 4, core: 2. Of those that a mesh axis runs over, the one named last changes fastest.
Arguments:
- volume: bfloat16 [4096, 256], P('slab'), may hold values from -6 to 6
- interp: bfloat16 [4, 8, 16, 4096], P('img', None, None, 'slab'), may hold values from -0.25 to 0.25
- block_index: int32 [4, 8, 8], P('img'), may hold values from 0 to 7
- images: bfloat16 [4, 128, 128, 256], P('img', 'slab'), may hold values from -6 to 6
- defocus: float32 [4, 128], P('img', 'slab'), may hold values from 5000 to 25000
- orient: int32 [4, 128, 4], P('img', 'slab'), may hold values from 0 to 7, all different within a row
Outputs:
- update: float32 [4096, 256], P('slab')
- weights: float32 [4, 128, 64], P('img', 'slab')
The draws below stay inside these ranges and needn't reach their ends.
Inputs may be any that keep to these rules, and one draw needn't show every extreme that they name: `orient`: each image lists 4 different orientations of its group.
All inputs are finite; a program needn't handle non-finite values.
Results may differ from the reference program's by a relative error of at most 0.0077.
Values may be sent and summed in bfloat16 or wider, within the bound.
No kernel may reach another device: no remote copies, remote signals or barrier semaphores. Data moves between devices by JAX's collectives and lax.ppermute only.
A program may use at most 64 MiB of HBM per device.

```python
import math
import jax
import jax.numpy as jnp
from jax import lax

CUR = 128
BOX = 256
PB = 16
ROWS_SLAB = 512
TOPK = 4
NS = 16
NSLAB = 8
NGRP = 4
OGRP = 8
IMAGES_G = 128
VROWS = 4096
NBLK = 8
N_SLAB = 8


def touch_ends(values, rng, low, largest):
    longest = values.shape.index(max(values.shape))
    spots = []
    for shift in (0, 1):
        where = [jax.random.randint(jax.random.fold_in(rng, axis), (), 0, length) for axis, length in enumerate(values.shape)]
        where[longest] = (where[longest] + shift) % values.shape[longest]
        spots.append(tuple(where))
    return values.at[spots[0]].set(low).at[spots[1]].set(largest)


def shard_levels(rng, dims, shards, least, top_value):
    def one(axis_at, shards_of):
        steps = jax.random.uniform(jax.random.fold_in(jax.random.fold_in(rng, 6), axis_at), (shards_of,), jnp.float32, least / len(shards), top_value / len(shards))
        return jnp.repeat(jnp.exp(steps), dims[axis_at] // shards_of).reshape((-1,) + (1,) * (len(dims) - axis_at - 1))

    gain = one(*shards[0])
    for cut in shards[1:]:
        gain = gain * one(*cut)
    return gain


def distinct(own_key, rows, number_of, top, lift):
    order = jax.random.permutation(jax.random.fold_in(own_key, 1), number_of)
    boost = order
    for power in range(3):
        boost = boost * boost // number_of
    boost = boost * lift // number_of
    chance = jax.random.randint(jax.random.fold_in(own_key, 2), (rows, number_of), 0, 4096) + boost
    sure = jax.random.permutation(jax.random.fold_in(own_key, 3), rows)[jnp.arange(number_of) % rows]
    chance = jnp.where(jnp.arange(rows)[:, None] == sure[None, :], 1 << 14, chance)
    score = chance * number_of + jnp.arange(number_of)
    return lax.top_k(score.astype(jnp.int32), top)[1].astype(jnp.int32)


def normal_values(key, dims, width, reach, shards=(), held_as=jnp.bfloat16):
    entries = width * jax.random.normal(key, dims, jnp.float32)
    if shards:
        entries = entries * shard_levels(key, dims, shards, -0.22, 0.18)
    return jnp.clip(entries, -reach, reach).astype(held_as)


def setup_inputs(seed: int = 0) -> dict:
    splits = jax.random.split(jax.random.key(seed), 7)
    volume = normal_values(splits[0], (VROWS, 2 * CUR), 1.0, 6.0, ((0, 8),))
    interp = normal_values(splits[1], (NGRP, OGRP, PB, VROWS), (ROWS_SLAB * N_SLAB * PB // CUR) ** -0.5, 0.25, ((0, 4), (3, 8)))
    block_index = touch_ends(jax.random.randint(splits[2], (NGRP, OGRP, NSLAB), 0, NBLK), jax.random.fold_in(splits[2], 1), 0, NBLK - 1).astype(jnp.int32)
    images = normal_values(splits[3], (NGRP, IMAGES_G, CUR, 2 * CUR), 1.0, 6.0, ((0, 4), (1, 8)))
    defocus = jnp.clip(5000.0 + 20000.0 * jax.random.uniform(splits[4], (NGRP, IMAGES_G), jnp.float32) ** shard_levels(splits[4], (NGRP, IMAGES_G), ((0, 4), (1, 8)), -0.2, 0.2), 5000.0, 25000.0)
    orient = distinct(splits[5], NGRP * IMAGES_G, OGRP, TOPK, 8192).reshape((NGRP, IMAGES_G, TOPK))
    return {"volume": volume, "interp": interp, "block_index": block_index, "images": images, "defocus": defocus, "orient": orient}


wave_length = 0.0197
aberration = 27000000.0
amplitude = 0.1
grid_side = 4

def phase_tables(fourier, shifts, box):
    freq = (jnp.arange(fourier, dtype=jnp.int32) - fourier // 2).astype(jnp.float32)
    shift_steps = jnp.arange(shifts, dtype=jnp.int32)
    shift_x = (2 * (shift_steps // grid_side) - (grid_side - 1)).astype(jnp.float32)
    shift_y = (2 * (shift_steps % grid_side) - (grid_side - 1)).astype(jnp.float32)
    angle = 2.0 * math.pi / box * (freq[:, None, None] * shift_x + freq[None, :, None] * shift_y)
    forward = jnp.stack([jnp.cos(angle), jnp.sin(angle)], axis=1).reshape(2 * fourier * fourier, shifts)
    backward = jnp.stack([jnp.cos(angle), -jnp.sin(angle)], axis=1).reshape(2 * fourier * fourier, shifts)
    return (forward.astype(jnp.bfloat16), backward.T.astype(jnp.bfloat16))

def contrast(defocus_blk, fourier, box):
    freq = (jnp.arange(fourier, dtype=jnp.int32) - fourier // 2).astype(jnp.float32)
    wave_sq = (freq[:, None] * freq[:, None] + freq[None, :] * freq[None, :]) / (box * box)
    phase = math.pi * wave_length * defocus_blk[:, None, None] * wave_sq
    phase = phase - 0.5 * math.pi * aberration * wave_length ** 3 * wave_sq * wave_sq
    return -(math.sqrt(1.0 - amplitude * amplitude) * jnp.sin(phase) + amplitude * jnp.cos(phase))

def correlate(panels, image_blk, list_blk, defocus_blk, phase_fwd, phase_back, box):
    count = image_blk.shape[0]
    fourier = image_blk.shape[1]
    picks = list_blk.shape[1]
    shifts = phase_fwd.shape[1]
    ctf = contrast(defocus_blk, fourier, box)
    weighted = ctf[:, :, None, :] * image_blk.astype(jnp.float32).reshape(count, fourier, 2, fourier)
    real_u = weighted[:, None, :, 0]
    imag_u = weighted[:, None, :, 1]
    chosen = panels[list_blk].astype(jnp.float32).reshape(count, picks, fourier, 2, fourier)
    real_p = chosen[:, :, :, 0]
    imag_p = chosen[:, :, :, 1]
    product = jnp.stack([real_p * real_u + imag_p * imag_u, real_p * imag_u - imag_p * real_u], axis=3)
    product = product.astype(jnp.bfloat16).reshape(count * picks, 2 * fourier * fourier)
    scores = jnp.dot(product, phase_fwd, preferred_element_type=jnp.float32) / fourier
    scores = scores.reshape(count, picks * shifts)
    squared = scores * scores
    weights = squared / (lax.optimization_barrier(jnp.mean(squared, axis=1, keepdims=True)) + 1e-05)
    rounded = weights.astype(jnp.bfloat16).reshape(count * picks, shifts)
    spread = jnp.dot(rounded, phase_back, preferred_element_type=jnp.float32)
    spread = spread.reshape(count, picks, fourier, 2, fourier)
    real_e = spread[:, :, :, 0]
    imag_e = spread[:, :, :, 1]
    backed = jnp.stack([real_u * real_e - imag_u * imag_e, real_u * imag_e + imag_u * real_e], axis=3)
    backed = backed.astype(jnp.bfloat16).reshape(count * picks, 2 * fourier * fourier)
    return (weights, backed)

def reference(volume, interp, block_index, images, defocus, orient):
    phase_fwd, phase_back = phase_tables(CUR, NS, BOX)
    levels = jnp.arange(NBLK, dtype=jnp.int32)
    stacked_vol = volume.astype(jnp.float32).reshape(NSLAB, ROWS_SLAB, 2 * CUR)
    block = math.gcd(IMAGES_G, 128)
    block_total = IMAGES_G // block
    columns = jnp.zeros((NSLAB, ROWS_SLAB, 2 * CUR), jnp.float32)
    weight_list = []
    for group in range(NGRP):
        inter_g = interp[group].astype(jnp.float32).reshape(OGRP, PB, NSLAB, ROWS_SLAB)
        partial_value = jnp.einsum('jpsr,srx->jspx', inter_g, stacked_vol, precision=lax.Precision.HIGHEST)
        onehot = (block_index[group][:, :, None] == levels).astype(jnp.float32)
        panels = jnp.einsum('jsb,jspx->jbpx', onehot, partial_value, precision=lax.Precision.HIGHEST)
        panels = panels.reshape(OGRP, CUR, 2 * CUR).astype(jnp.bfloat16)

        def step_fn(accum, pieces):
            image_blk, list_blk, defocus_blk = pieces
            weights, backed = correlate(panels, image_blk, list_blk, defocus_blk, phase_fwd, phase_back, BOX)
            accum = accum + jax.ops.segment_sum(backed.astype(jnp.float32), list_blk.reshape(-1), num_segments=OGRP)
            return (accum, weights)
        start = jnp.zeros((OGRP, 2 * CUR * CUR), jnp.float32)
        accum, weights = lax.scan(step_fn, start, (images[group].reshape(block_total, block, CUR, 2 * CUR), orient[group].reshape(block_total, block, TOPK), defocus[group].reshape(block_total, block)))
        weight_list.append(weights.reshape(IMAGES_G, TOPK * NS))
        back_slices = accum.astype(jnp.bfloat16).reshape(OGRP, NBLK, PB, 2 * CUR)
        taken = jnp.take_along_axis(back_slices, block_index[group][:, :, None, None], axis=1)
        columns = columns + jnp.einsum('jpsr,jspx->srx', inter_g, taken.astype(jnp.float32), precision=lax.Precision.HIGHEST)
    update = (columns / math.sqrt(IMAGES_G)).reshape(VROWS, 2 * CUR)
    return (update, jnp.stack(weight_list))
```

```python
import math

import jax
import jax.numpy as jnp
import numpy as np
from jax import lax
from jax.experimental import pallas as pl
from jax.experimental.pallas import tpu as pltpu
from jax.sharding import PartitionSpec as P

BOX = 256
NS = 16

wave_length = 0.0197
aberration = 27000000.0
amplitude = 0.1
grid_side = 4
LANES = 128
DIRECT_BYTES = 4 << 20


def split_bf16(values):
    high = values.astype(jnp.bfloat16)
    low = (values - high.astype(np.float64)).astype(jnp.bfloat16)
    return high, low


def separable_tables(fourier):
    freq = np.arange(fourier) - fourier // 2
    shift = np.arange(NS)
    shift_x = 2 * (shift // grid_side) - (grid_side - 1)
    shift_y = 2 * (shift % grid_side) - (grid_side - 1)
    row = 2.0 * math.pi / BOX * freq[:, None] * shift_x
    col = 2.0 * math.pi / BOX * freq[:, None] * shift_y
    row_table = np.concatenate([np.cos(row), np.sin(row)] * 4, axis=1).astype(np.float32)
    even = np.concatenate([np.cos(col), np.sin(col)], axis=0)
    odd = np.concatenate([-np.sin(col), np.cos(col)], axis=0)
    even_high, even_low = split_bf16(even)
    odd_high, odd_low = split_bf16(odd)
    col_fwd = np.concatenate([even_high, odd_high, even_low, odd_low] * 2, axis=1)
    even = np.concatenate([np.cos(col), -np.sin(col)], axis=0).T
    odd = np.concatenate([-np.sin(col), -np.cos(col)], axis=0).T
    even_high, even_low = split_bf16(even)
    odd_high, odd_low = split_bf16(odd)
    blank = np.zeros((LANES - 4 * NS, 2 * fourier), jnp.bfloat16)
    col_back = np.concatenate([even_high, odd_high, even_low, odd_low, blank], axis=0)
    return row_table, col_fwd, col_back


def contrast_tables(fourier):
    freq = np.arange(fourier) - fourier // 2
    wave_sq = (freq[:, None] ** 2 + freq[None, :] ** 2) / float(BOX * BOX)
    slope = wave_length * wave_sq / 2.0
    offset = -0.25 * aberration * wave_length**3 * wave_sq * wave_sq
    offset = offset + math.asin(amplitude) / (2.0 * math.pi)
    return slope.astype(np.float32), offset.astype(np.float32)


def sin_turns(turns):
    part = turns - jnp.round(turns)
    folded = jnp.where(part > 0.25, 0.5 - part, jnp.where(part < -0.25, -0.5 - part, part))
    x = folded * (2.0 * math.pi)
    y = x * x
    poly = -1.0 / 39916800.0
    for coefficient in (1.0 / 362880.0, -1.0 / 5040.0, 1.0 / 120.0, -1.0 / 6.0, 1.0):
        poly = poly * y + coefficient
    return x * poly


def weigh_images(slope, offset, images, defocus):
    count, fourier, width = images.shape

    def kernel(defocus_ref, slope_ref, offset_ref, image_ref, u_ref):
        def one(i, _):
            ctf = -sin_turns(defocus_ref[0, i] * slope_ref[...] + offset_ref[...])
            u_ref[i, :, :fourier] = ctf * image_ref[i, :, :fourier].astype(jnp.float32)
            u_ref[i, :, fourier:] = ctf * image_ref[i, :, fourier:].astype(jnp.float32)
            return 0

        lax.fori_loop(0, count, one, 0)

    return pl.pallas_call(
        kernel,
        out_shape=jax.ShapeDtypeStruct(images.shape, jnp.float32),
        in_specs=[pl.BlockSpec(memory_space=pltpu.SMEM)] + [pl.BlockSpec(memory_space=pltpu.VMEM)] * 3,
        out_specs=pl.BlockSpec(memory_space=pltpu.VMEM),
        compiler_params=pltpu.CompilerParams(vmem_limit_bytes=24 << 20),
        cost_estimate=pl.CostEstimate(
            flops=30 * count * fourier * fourier, bytes_accessed=6 * count * fourier * width, transcendentals=0
        ),
        name="weigh_images",
    )(defocus, slope, offset, images)


def expectation(tables, u, parts, slabs, block_index, orient):
    count, fourier, width = u.shape
    orient_count, block_rows, _ = parts[0].shape
    slab_count = len(parts)
    picks = orient.shape[1]
    row_table, col_fwd, col_back = tables

    def kernel(slabs_ref, index_ref, orient_ref, row_ref, fwd_ref, back_ref, u_ref, *rest):
        part_refs = rest[:slab_count]
        weights_ref, rows_ref, panel, total, score = rest[slab_count:]
        panel[...] = jnp.zeros_like(panel)
        for part in range(slab_count):
            slab = slabs_ref[part]
            for j in range(orient_count):
                where = pl.ds(pl.multiple_of(index_ref[j, slab] * block_rows, block_rows), block_rows)
                panel[j, where, :] += part_refs[part][j].astype(jnp.float32)
        for j in range(orient_count):
            panel[j] = panel[j].astype(jnp.bfloat16).astype(jnp.float32)
        total[...] = jnp.zeros_like(total)

        def forward(i, _):
            real_u = u_ref[i, :, :fourier]
            imag_u = u_ref[i, :, fourier:]
            products = []
            for k in range(picks):
                j = orient_ref[i, k]
                real_p = panel[j, :, :fourier]
                imag_p = panel[j, :, fourier:]
                products.append(
                    jnp.concatenate(
                        [
                            (real_p * real_u + imag_p * imag_u).astype(jnp.bfloat16),
                            (real_p * imag_u - imag_p * real_u).astype(jnp.bfloat16),
                        ],
                        axis=1,
                    )
                )
            by_row = jnp.dot(
                jnp.concatenate(products, axis=0), fwd_ref[...], preferred_element_type=jnp.float32
            )
            for k in range(picks):
                mixed = by_row[k * fourier : (k + 1) * fourier] * row_ref[...]
                score[k, pl.ds(i, 1), :] = jnp.sum(mixed, axis=0, keepdims=True)
            return 0

        lax.fori_loop(0, count, forward, 0)

        squared = []
        for k in range(picks):
            value = score[k]
            value = value + pltpu.roll(value, 2 * NS, 1)
            value = value + pltpu.roll(value, NS, 1)
            value = value * (1.0 / fourier)
            squared.append(value * value)
        mean = jnp.sum(sum(squared), axis=1, keepdims=True) * (1.0 / (LANES * picks))
        scale = 1.0 / (mean + 1e-05)
        lane = lax.broadcasted_iota(jnp.int32, (count, LANES), 1) // NS
        merged = jnp.zeros((count, LANES), jnp.float32)
        for k in range(picks):
            value = squared[k] * scale
            merged = jnp.where(lane == k, value, merged)
            score[k] = value.astype(jnp.bfloat16).astype(jnp.float32)
        weights_ref[...] = merged[:, : picks * NS]

        def backward(i, _):
            real_u = u_ref[i, :, :fourier]
            imag_u = u_ref[i, :, fourier:]
            mixed = [(row_ref[...] * score[k, pl.ds(i, 1), :]).astype(jnp.bfloat16) for k in range(picks)]
            spread = jnp.dot(jnp.concatenate(mixed, axis=0), back_ref[...], preferred_element_type=jnp.float32)
            for k in range(picks):
                j = orient_ref[i, k]
                real_e = spread[k * fourier : (k + 1) * fourier, :fourier]
                imag_e = spread[k * fourier : (k + 1) * fourier, fourier:]
                total[j, :, :fourier] += real_u * real_e - imag_u * imag_e
                total[j, :, fourier:] += real_u * imag_e + imag_u * real_e
            return 0

        lax.fori_loop(0, count, backward, 0)

        for slab in range(slab_count):
            for j in range(orient_count):
                where = pl.ds(pl.multiple_of(index_ref[j, slab] * block_rows, block_rows), block_rows)
                rows_ref[slab, j] = total[j, where, :].astype(jnp.bfloat16)

    smem = pl.BlockSpec(memory_space=pltpu.SMEM)
    vmem = pl.BlockSpec(memory_space=pltpu.VMEM)
    return pl.pallas_call(
        kernel,
        out_shape=(
            jax.ShapeDtypeStruct((count, picks * NS), jnp.float32),
            jax.ShapeDtypeStruct((slab_count, orient_count, block_rows, width), jnp.bfloat16),
        ),
        in_specs=[smem] * 3 + [vmem] * (4 + slab_count),
        out_specs=(vmem, vmem),
        scratch_shapes=[
            pltpu.VMEM((orient_count, fourier, width), jnp.float32),
            pltpu.VMEM((orient_count, fourier, width), jnp.float32),
            pltpu.VMEM((picks, count, LANES), jnp.float32),
        ],
        compiler_params=pltpu.CompilerParams(vmem_limit_bytes=32 << 20),
        cost_estimate=pl.CostEstimate(
            flops=64 * count * picks * fourier * width, bytes_accessed=6 * count * fourier * width, transcendentals=0
        ),
        name="expectation",
    )(slabs, block_index, orient, row_table, col_fwd, col_back, u, *parts)


def exchange(value, axis, size):
    return [
        lax.ppermute(value, axis, [(source, (source + step) % size) for source in range(size)])
        for step in range(1, size)
    ]


def direct(volume, interp, block_index, images, defocus, orient):
    slab_count = lax.axis_size("slab")
    group_count = lax.axis_size("img")
    slab_index = lax.axis_index("slab")
    orient_count, block_rows, slab_rows = interp.shape[1:]
    fourier = images.shape[2]
    width = images.shape[3]
    image_count = images.shape[1] * slab_count
    weigher = interp[0].reshape(orient_count * block_rows, slab_rows)
    partial_value = jnp.dot(weigher, volume, preferred_element_type=jnp.float32).astype(jnp.bfloat16)
    partial_value = partial_value.reshape(orient_count, block_rows, width)
    parts = [partial_value] + exchange(partial_value, "slab", slab_count)
    slabs = lax.rem(slab_index - jnp.arange(slab_count, dtype=jnp.int32) + slab_count, slab_count)
    weighers = [weigher] + exchange(weigher, "img", group_count)
    slope, offset = contrast_tables(fourier)
    u = weigh_images(slope, offset, images[0], defocus)
    weights, rows = expectation(separable_tables(fourier), u, parts, slabs, block_index[0], orient[0])
    arrived = lax.all_to_all(rows, "slab", split_axis=0, concat_axis=0, tiled=True)
    back = jnp.sum(arrived.astype(jnp.float32), axis=0).astype(jnp.bfloat16)
    back = back.reshape(orient_count * block_rows, width)
    backs = [back] + exchange(back, "img", group_count)
    update = lax.dot_general(
        jnp.concatenate(weighers, axis=0),
        jnp.concatenate(backs, axis=0),
        (((0,), (0,)), ((), ())),
        preferred_element_type=jnp.float32,
    )
    return update / math.sqrt(image_count), weights[None]


def phase_tables(fourier, shifts, box):
    freq = (jnp.arange(fourier, dtype=jnp.int32) - fourier // 2).astype(jnp.float32)
    shift_steps = jnp.arange(shifts, dtype=jnp.int32)
    shift_x = (2 * (shift_steps // grid_side) - (grid_side - 1)).astype(jnp.float32)
    shift_y = (2 * (shift_steps % grid_side) - (grid_side - 1)).astype(jnp.float32)
    angle = 2.0 * math.pi / box * (freq[:, None, None] * shift_x + freq[None, :, None] * shift_y)
    forward = jnp.stack([jnp.cos(angle), jnp.sin(angle)], axis=1).reshape(
        2 * fourier * fourier, shifts
    )
    backward = jnp.stack([jnp.cos(angle), -jnp.sin(angle)], axis=1).reshape(
        2 * fourier * fourier, shifts
    )
    return (forward.astype(jnp.bfloat16), backward.T.astype(jnp.bfloat16))


def contrast(defocus_blk, fourier, box):
    freq = (jnp.arange(fourier, dtype=jnp.int32) - fourier // 2).astype(jnp.float32)
    wave_sq = (freq[:, None] * freq[:, None] + freq[None, :] * freq[None, :]) / (box * box)
    phase = math.pi * wave_length * defocus_blk[:, None, None] * wave_sq
    phase = phase - 0.5 * math.pi * aberration * wave_length**3 * wave_sq * wave_sq
    return -(math.sqrt(1.0 - amplitude * amplitude) * jnp.sin(phase) + amplitude * jnp.cos(phase))


def correlate(panels, image_blk, list_blk, defocus_blk, phase_fwd, phase_back, box):
    count = image_blk.shape[0]
    fourier = image_blk.shape[1]
    picks = list_blk.shape[1]
    shifts = phase_fwd.shape[1]
    ctf = contrast(defocus_blk, fourier, box)
    weighted = ctf[:, :, None, :] * image_blk.astype(jnp.float32).reshape(
        count, fourier, 2, fourier
    )
    real_u = weighted[:, None, :, 0]
    imag_u = weighted[:, None, :, 1]
    chosen = panels[list_blk].astype(jnp.float32).reshape(count, picks, fourier, 2, fourier)
    real_p = chosen[:, :, :, 0]
    imag_p = chosen[:, :, :, 1]
    product = jnp.stack(
        [real_p * real_u + imag_p * imag_u, real_p * imag_u - imag_p * real_u], axis=3
    )
    product = product.astype(jnp.bfloat16).reshape(count * picks, 2 * fourier * fourier)
    scores = jnp.dot(product, phase_fwd, preferred_element_type=jnp.float32) / fourier
    scores = scores.reshape(count, picks * shifts)
    squared = scores * scores
    weights = squared / (jnp.mean(squared, axis=1, keepdims=True) + 1e-05)
    rounded = weights.astype(jnp.bfloat16).reshape(count * picks, shifts)
    spread = jnp.dot(rounded, phase_back, preferred_element_type=jnp.float32)
    spread = spread.reshape(count, picks, fourier, 2, fourier)
    real_e = spread[:, :, :, 0]
    imag_e = spread[:, :, :, 1]
    backed = jnp.stack(
        [real_u * real_e - imag_u * imag_e, real_u * imag_e + imag_u * real_e], axis=3
    )
    backed = backed.astype(jnp.bfloat16).reshape(count * picks, 2 * fourier * fourier)
    return (weights, backed)


def through_owners(volume, interp, block_index, images, defocus, orient):
    slab_count = lax.axis_size("slab")
    slab_index = lax.axis_index("slab")
    orient_count = interp.shape[1]
    ori_dev = orient_count // slab_count
    block_rows = interp.shape[2]
    fourier = images.shape[2]
    block_count = fourier // block_rows
    img_dev = images.shape[1]
    picks = orient.shape[2]
    levels = jnp.arange(block_count, dtype=jnp.int32)
    partial_value = jnp.einsum("jpr,rx->jpx", interp[0], volume, preferred_element_type=jnp.float32)
    owned_idx = lax.dynamic_slice_in_dim(block_index[0], slab_index * ori_dev, ori_dev, 0)
    arrived = lax.all_to_all(partial_value, "slab", split_axis=0, concat_axis=0, tiled=True)
    arrived = arrived.reshape(slab_count, ori_dev, block_rows, 2 * fourier)
    chosen = (owned_idx[:, :, None] == levels).astype(jnp.float32)
    summed = jnp.einsum("osb,sopx->obpx", chosen, arrived, precision=lax.Precision.HIGHEST)
    summed = summed.reshape(ori_dev, fourier, 2 * fourier)
    panels = lax.all_gather(summed.astype(jnp.bfloat16), "slab", axis=0, tiled=True)
    phase_fwd, phase_back = phase_tables(fourier, NS, BOX)
    blk = math.gcd(img_dev, 32)
    blk_total = img_dev // blk

    def per_block(pieces):
        image_blk, list_blk, defocus_blk = pieces
        return correlate(panels, image_blk, list_blk, defocus_blk, phase_fwd, phase_back, BOX)

    weights, backs = lax.map(
        per_block,
        (
            images[0].reshape(blk_total, blk, fourier, 2 * fourier),
            orient[0].reshape(blk_total, blk, picks),
            defocus[0].reshape(blk_total, blk),
        ),
    )
    all_slices = backs.reshape(img_dev * picks, 2 * fourier * fourier)
    member = (
        orient[0].reshape(-1)[:, None] == jnp.arange(orient_count, dtype=jnp.int32)[None, :]
    ).astype(jnp.bfloat16)
    back_own = lax.psum_scatter(
        lax.dot_general(
            member, all_slices, (((0,), (0,)), ((), ())), preferred_element_type=jnp.float32
        ),
        "slab",
        scatter_dimension=0,
        tiled=True,
    ).astype(jnp.bfloat16)
    back_own = back_own.reshape(ori_dev, block_count, block_rows, 2 * fourier)
    chosen_back = (owned_idx[:, :, None] == levels).astype(jnp.bfloat16)
    outgoing = jnp.einsum(
        "osb,obpx->sopx", chosen_back, back_own, preferred_element_type=jnp.float32
    )
    outgoing = outgoing.astype(jnp.bfloat16).reshape(slab_count * ori_dev, block_rows, 2 * fourier)
    incoming = lax.all_to_all(outgoing, "slab", split_axis=0, concat_axis=0, tiled=True)
    column = jnp.einsum("jpr,jpx->rx", interp[0], incoming, preferred_element_type=jnp.float32)
    summed_cols = lax.psum(column, "img")
    update = summed_cols / math.sqrt(img_dev * slab_count)
    return (update, weights)


def on_device(volume, interp, block_index, images, defocus, orient):
    orient_count, block_rows = interp.shape[1:3]
    gathered = lax.axis_size("slab") * orient_count * block_rows * images.shape[3] * 2
    plan = direct if gathered <= DIRECT_BYTES else through_owners
    return plan(volume, interp, block_index, images, defocus, orient)


def solution(mesh):
    return jax.shard_map(
        on_device,
        mesh=mesh,
        in_specs=(
            P("slab", None),
            P("img", None, None, "slab"),
            P("img", None, None),
            P("img", "slab", None, None),
            P("img", "slab"),
            P("img", "slab", None),
        ),
        out_specs=(P("slab", None), P("img", "slab", None)),
        check_vma=False,
    )
```

```python
import math

import jax
import jax.numpy as jnp
import numpy as np
from jax import lax
from jax.experimental import pallas as pl
from jax.experimental.pallas import tpu as pltpu
from jax.sharding import PartitionSpec as P

BOX = 256
NS = 16

wave_length = 0.0197
aberration = 27000000.0
amplitude = 0.1
grid_side = 4
LANES = 128
DIRECT_BYTES = 4 << 20


def split_bf16(values):
    high = values.astype(jnp.bfloat16)
    low = (values - high.astype(np.float64)).astype(jnp.bfloat16)
    return high, low


def separable_tables(fourier):
    freq = np.arange(fourier) - fourier // 2
    shift = np.arange(NS)
    shift_x = 2 * (shift // grid_side) - (grid_side - 1)
    shift_y = 2 * (shift % grid_side) - (grid_side - 1)
    row = 2.0 * math.pi / BOX * freq[:, None] * shift_x
    col = 2.0 * math.pi / BOX * freq[:, None] * shift_y
    row_table = np.concatenate([np.cos(row), np.sin(row)] * 4, axis=1).astype(np.float32)
    even = np.concatenate([np.cos(col), np.sin(col)], axis=0)
    odd = np.concatenate([-np.sin(col), np.cos(col)], axis=0)
    even_high, even_low = split_bf16(even)
    odd_high, odd_low = split_bf16(odd)
    col_fwd = np.concatenate([even_high, odd_high, even_low, odd_low] * 2, axis=1)
    even = np.concatenate([np.cos(col), -np.sin(col)], axis=0).T
    odd = np.concatenate([-np.sin(col), -np.cos(col)], axis=0).T
    even_high, even_low = split_bf16(even)
    odd_high, odd_low = split_bf16(odd)
    blank = np.zeros((LANES - 4 * NS, 2 * fourier), jnp.bfloat16)
    col_back = np.concatenate([even_high, odd_high, even_low, odd_low, blank], axis=0)
    return row_table, col_fwd, col_back


def sin_turns(turns):
    part = turns - jnp.round(turns)
    folded = jnp.where(part > 0.25, 0.5 - part, jnp.where(part < -0.25, -0.5 - part, part))
    x = folded * (2.0 * math.pi)
    y = x * x
    poly = -1.0 / 39916800.0
    for coefficient in (1.0 / 362880.0, -1.0 / 5040.0, 1.0 / 120.0, -1.0 / 6.0, 1.0):
        poly = poly * y + coefficient
    return x * poly


def weigh_images(images, defocus):
    _, count, fourier, width = images.shape

    def kernel(defocus_ref, image_ref, u_ref):
        kx = lax.broadcasted_iota(jnp.int32, (fourier, fourier), 0) - fourier // 2
        ky = lax.broadcasted_iota(jnp.int32, (fourier, fourier), 1) - fourier // 2
        wave_sq = (kx * kx + ky * ky).astype(jnp.float32) * (1.0 / (BOX * BOX))
        slope = wave_sq * (0.5 * wave_length)
        offset = wave_sq * wave_sq * (-0.25 * aberration * wave_length**3)
        offset = offset + math.asin(amplitude) / (2.0 * math.pi)
        for i in range(count):
            ctf = -sin_turns(defocus_ref[0, i] * slope + offset)
            u_ref[i, :, :fourier] = ctf * image_ref[0, i, :, :fourier].astype(jnp.float32)
            u_ref[i, :, fourier:] = ctf * image_ref[0, i, :, fourier:].astype(jnp.float32)

    return pl.pallas_call(
        kernel,
        out_shape=jax.ShapeDtypeStruct(images.shape[1:], jnp.float32),
        in_specs=[pl.BlockSpec(memory_space=pltpu.SMEM), pl.BlockSpec(memory_space=pltpu.VMEM)],
        out_specs=pl.BlockSpec(memory_space=pltpu.VMEM),
        compiler_params=pltpu.CompilerParams(vmem_limit_bytes=24 << 20),
        cost_estimate=pl.CostEstimate(
            flops=30 * count * fourier * fourier, bytes_accessed=6 * count * fourier * width, transcendentals=0
        ),
        name="weigh_images",
    )(defocus, images)


def expectation(tables, u, parts, slabs, block_index, orient):
    count, fourier, width = u.shape
    orient_count, block_rows, _ = parts[0].shape
    slab_count = len(parts)
    picks = orient.shape[0]
    row_table, col_fwd, col_back = tables

    def kernel(slabs_ref, index_ref, orient_ref, row_ref, fwd_ref, back_ref, u_ref, *rest):
        part_refs = rest[:slab_count]
        weights_ref, rows_ref, panel, total, score = rest[slab_count:]
        panel[...] = jnp.zeros_like(panel)
        for part in range(slab_count):
            slab = slabs_ref[part]
            for j in range(orient_count):
                where = pl.ds(pl.multiple_of(index_ref[j, slab] * block_rows, block_rows), block_rows)
                panel[j, where, :] += part_refs[part][j].astype(jnp.float32)
        for j in range(orient_count):
            panel[j] = panel[j].astype(jnp.bfloat16).astype(jnp.float32)
        total[...] = jnp.zeros_like(total)

        def forward(i, _):
            real_u = u_ref[i, :, :fourier]
            imag_u = u_ref[i, :, fourier:]
            products = []
            for k in range(picks):
                j = orient_ref[k, i]
                real_p = panel[j, :, :fourier]
                imag_p = panel[j, :, fourier:]
                products.append(
                    jnp.concatenate(
                        [
                            (real_p * real_u + imag_p * imag_u).astype(jnp.bfloat16),
                            (real_p * imag_u - imag_p * real_u).astype(jnp.bfloat16),
                        ],
                        axis=1,
                    )
                )
            by_row = jnp.dot(
                jnp.concatenate(products, axis=0), fwd_ref[...], preferred_element_type=jnp.float32
            )
            for k in range(picks):
                mixed = by_row[k * fourier : (k + 1) * fourier] * row_ref[...]
                score[k, pl.ds(i, 1), :] = jnp.sum(mixed, axis=0, keepdims=True)
            return 0

        lax.fori_loop(0, count, forward, 0, unroll=True)

        squared = []
        for k in range(picks):
            value = score[k]
            value = value + pltpu.roll(value, 2 * NS, 1)
            value = value + pltpu.roll(value, NS, 1)
            value = value * (1.0 / fourier)
            squared.append(value * value)
        mean = jnp.sum(sum(squared), axis=1, keepdims=True) * (1.0 / (LANES * picks))
        scale = 1.0 / (mean + 1e-05)
        lane = lax.broadcasted_iota(jnp.int32, (count, LANES), 1) // NS
        merged = jnp.zeros((count, LANES), jnp.float32)
        for k in range(picks):
            value = squared[k] * scale
            merged = jnp.where(lane == k, value, merged)
            score[k] = value.astype(jnp.bfloat16).astype(jnp.float32)
        weights_ref[...] = merged[:, : picks * NS]

        def backward(i, _):
            real_u = u_ref[i, :, :fourier]
            imag_u = u_ref[i, :, fourier:]
            mixed = [(row_ref[...] * score[k, pl.ds(i, 1), :]).astype(jnp.bfloat16) for k in range(picks)]
            spread = jnp.dot(jnp.concatenate(mixed, axis=0), back_ref[...], preferred_element_type=jnp.float32)
            for k in range(picks):
                j = orient_ref[k, i]
                real_e = spread[k * fourier : (k + 1) * fourier, :fourier]
                imag_e = spread[k * fourier : (k + 1) * fourier, fourier:]
                total[j, :, :fourier] += real_u * real_e - imag_u * imag_e
                total[j, :, fourier:] += real_u * imag_e + imag_u * real_e
            return 0

        lax.fori_loop(0, count, backward, 0, unroll=True)

        for slab in range(slab_count):
            for j in range(orient_count):
                where = pl.ds(pl.multiple_of(index_ref[j, slab] * block_rows, block_rows), block_rows)
                rows_ref[slab, j] = total[j, where, :].astype(jnp.bfloat16)

    smem = pl.BlockSpec(memory_space=pltpu.SMEM)
    vmem = pl.BlockSpec(memory_space=pltpu.VMEM)
    return pl.pallas_call(
        kernel,
        out_shape=(
            jax.ShapeDtypeStruct((count, picks * NS), jnp.float32),
            jax.ShapeDtypeStruct((slab_count, orient_count, block_rows, width), jnp.bfloat16),
        ),
        in_specs=[smem] * 3 + [vmem] * (4 + slab_count),
        out_specs=(vmem, vmem),
        scratch_shapes=[
            pltpu.VMEM((orient_count, fourier, width), jnp.float32),
            pltpu.VMEM((orient_count, fourier, width), jnp.float32),
            pltpu.VMEM((picks, count, LANES), jnp.float32),
        ],
        compiler_params=pltpu.CompilerParams(vmem_limit_bytes=32 << 20),
        cost_estimate=pl.CostEstimate(
            flops=64 * count * picks * fourier * width, bytes_accessed=6 * count * fourier * width, transcendentals=0
        ),
        name="expectation",
    )(slabs, block_index, orient, row_table, col_fwd, col_back, u, *parts)


def exchange(value, axis, size):
    return [
        lax.ppermute(value, axis, [(source, (source + step) % size) for source in range(size)])
        for step in range(1, size)
    ]


def swap(value, axis, size, flip):
    return lax.ppermute(value, axis, [(source, source ^ flip) for source in range(size)])


def direct(volume, interp, block_index, images, defocus, orient):
    slab_count = lax.axis_size("slab")
    group_count = lax.axis_size("img")
    slab_index = lax.axis_index("slab")
    orient_count, block_rows, slab_rows = interp.shape[1:]
    fourier = images.shape[2]
    width = images.shape[3]
    image_count = images.shape[1] * slab_count
    weigher = interp[0].reshape(orient_count * block_rows, slab_rows)
    partial_value = jnp.dot(weigher, volume, preferred_element_type=jnp.float32).astype(jnp.bfloat16)
    partial_value = partial_value.reshape(orient_count, block_rows, width)
    same_x = [partial_value] + [swap(partial_value, "slab", slab_count, flip) for flip in range(2, slab_count, 2)]
    other_x = [swap(partial_value, "slab", slab_count, 1)]
    passed_on = swap(jnp.stack(same_x[1:]), "slab", slab_count, 1)
    other_x += [passed_on[i] for i in range(slab_count // 2 - 1)]
    parts = same_x + other_x
    flips = list(range(0, slab_count, 2)) + list(range(1, slab_count, 2))
    slabs = jnp.bitwise_xor(slab_index, jnp.array(flips, jnp.int32))
    weighers = [weigher] + exchange(weigher, "img", group_count)
    u = weigh_images(images, defocus)
    weights, rows = expectation(separable_tables(fourier), u, parts, slabs, block_index[0], orient[0].T)
    arrived = lax.all_to_all(rows, "slab", split_axis=0, concat_axis=0, tiled=True)
    back = jnp.sum(arrived.astype(jnp.float32), axis=0).astype(jnp.bfloat16)
    back = back.reshape(orient_count * block_rows, width)
    backs = [back] + exchange(back, "img", group_count)
    update = lax.dot_general(
        jnp.concatenate(weighers, axis=0),
        jnp.concatenate(backs, axis=0),
        (((0,), (0,)), ((), ())),
        preferred_element_type=jnp.float32,
    )
    return update / math.sqrt(image_count), weights[None]


def phase_tables(fourier, shifts, box):
    freq = (jnp.arange(fourier, dtype=jnp.int32) - fourier // 2).astype(jnp.float32)
    shift_steps = jnp.arange(shifts, dtype=jnp.int32)
    shift_x = (2 * (shift_steps // grid_side) - (grid_side - 1)).astype(jnp.float32)
    shift_y = (2 * (shift_steps % grid_side) - (grid_side - 1)).astype(jnp.float32)
    angle = 2.0 * math.pi / box * (freq[:, None, None] * shift_x + freq[None, :, None] * shift_y)
    forward = jnp.stack([jnp.cos(angle), jnp.sin(angle)], axis=1).reshape(
        2 * fourier * fourier, shifts
    )
    backward = jnp.stack([jnp.cos(angle), -jnp.sin(angle)], axis=1).reshape(
        2 * fourier * fourier, shifts
    )
    return (forward.astype(jnp.bfloat16), backward.T.astype(jnp.bfloat16))


def contrast(defocus_blk, fourier, box):
    freq = (jnp.arange(fourier, dtype=jnp.int32) - fourier // 2).astype(jnp.float32)
    wave_sq = (freq[:, None] * freq[:, None] + freq[None, :] * freq[None, :]) / (box * box)
    phase = math.pi * wave_length * defocus_blk[:, None, None] * wave_sq
    phase = phase - 0.5 * math.pi * aberration * wave_length**3 * wave_sq * wave_sq
    return -(math.sqrt(1.0 - amplitude * amplitude) * jnp.sin(phase) + amplitude * jnp.cos(phase))


def correlate(panels, image_blk, list_blk, defocus_blk, phase_fwd, phase_back, box):
    count = image_blk.shape[0]
    fourier = image_blk.shape[1]
    picks = list_blk.shape[1]
    shifts = phase_fwd.shape[1]
    ctf = contrast(defocus_blk, fourier, box)
    weighted = ctf[:, :, None, :] * image_blk.astype(jnp.float32).reshape(
        count, fourier, 2, fourier
    )
    real_u = weighted[:, None, :, 0]
    imag_u = weighted[:, None, :, 1]
    chosen = panels[list_blk].astype(jnp.float32).reshape(count, picks, fourier, 2, fourier)
    real_p = chosen[:, :, :, 0]
    imag_p = chosen[:, :, :, 1]
    product = jnp.stack(
        [real_p * real_u + imag_p * imag_u, real_p * imag_u - imag_p * real_u], axis=3
    )
    product = product.astype(jnp.bfloat16).reshape(count * picks, 2 * fourier * fourier)
    scores = jnp.dot(product, phase_fwd, preferred_element_type=jnp.float32) / fourier
    scores = scores.reshape(count, picks * shifts)
    squared = scores * scores
    weights = squared / (jnp.mean(squared, axis=1, keepdims=True) + 1e-05)
    rounded = weights.astype(jnp.bfloat16).reshape(count * picks, shifts)
    spread = jnp.dot(rounded, phase_back, preferred_element_type=jnp.float32)
    spread = spread.reshape(count, picks, fourier, 2, fourier)
    real_e = spread[:, :, :, 0]
    imag_e = spread[:, :, :, 1]
    backed = jnp.stack(
        [real_u * real_e - imag_u * imag_e, real_u * imag_e + imag_u * real_e], axis=3
    )
    backed = backed.astype(jnp.bfloat16).reshape(count * picks, 2 * fourier * fourier)
    return (weights, backed)


def through_owners(volume, interp, block_index, images, defocus, orient):
    slab_count = lax.axis_size("slab")
    slab_index = lax.axis_index("slab")
    orient_count = interp.shape[1]
    ori_dev = orient_count // slab_count
    block_rows = interp.shape[2]
    fourier = images.shape[2]
    block_count = fourier // block_rows
    img_dev = images.shape[1]
    picks = orient.shape[2]
    levels = jnp.arange(block_count, dtype=jnp.int32)
    partial_value = jnp.einsum("jpr,rx->jpx", interp[0], volume, preferred_element_type=jnp.float32)
    owned_idx = lax.dynamic_slice_in_dim(block_index[0], slab_index * ori_dev, ori_dev, 0)
    arrived = lax.all_to_all(partial_value, "slab", split_axis=0, concat_axis=0, tiled=True)
    arrived = arrived.reshape(slab_count, ori_dev, block_rows, 2 * fourier)
    chosen = (owned_idx[:, :, None] == levels).astype(jnp.float32)
    summed = jnp.einsum("osb,sopx->obpx", chosen, arrived, precision=lax.Precision.HIGHEST)
    summed = summed.reshape(ori_dev, fourier, 2 * fourier)
    panels = lax.all_gather(summed.astype(jnp.bfloat16), "slab", axis=0, tiled=True)
    phase_fwd, phase_back = phase_tables(fourier, NS, BOX)
    blk = math.gcd(img_dev, 32)
    blk_total = img_dev // blk

    def per_block(pieces):
        image_blk, list_blk, defocus_blk = pieces
        return correlate(panels, image_blk, list_blk, defocus_blk, phase_fwd, phase_back, BOX)

    weights, backs = lax.map(
        per_block,
        (
            images[0].reshape(blk_total, blk, fourier, 2 * fourier),
            orient[0].reshape(blk_total, blk, picks),
            defocus[0].reshape(blk_total, blk),
        ),
    )
    all_slices = backs.reshape(img_dev * picks, 2 * fourier * fourier)
    member = (
        orient[0].reshape(-1)[:, None] == jnp.arange(orient_count, dtype=jnp.int32)[None, :]
    ).astype(jnp.bfloat16)
    back_own = lax.psum_scatter(
        lax.dot_general(
            member, all_slices, (((0,), (0,)), ((), ())), preferred_element_type=jnp.float32
        ),
        "slab",
        scatter_dimension=0,
        tiled=True,
    ).astype(jnp.bfloat16)
    back_own = back_own.reshape(ori_dev, block_count, block_rows, 2 * fourier)
    chosen_back = (owned_idx[:, :, None] == levels).astype(jnp.bfloat16)
    outgoing = jnp.einsum(
        "osb,obpx->sopx", chosen_back, back_own, preferred_element_type=jnp.float32
    )
    outgoing = outgoing.astype(jnp.bfloat16).reshape(slab_count * ori_dev, block_rows, 2 * fourier)
    incoming = lax.all_to_all(outgoing, "slab", split_axis=0, concat_axis=0, tiled=True)
    column = jnp.einsum("jpr,jpx->rx", interp[0], incoming, preferred_element_type=jnp.float32)
    summed_cols = lax.psum(column, "img")
    update = summed_cols / math.sqrt(img_dev * slab_count)
    return (update, weights)


def on_device(volume, interp, block_index, images, defocus, orient):
    orient_count, block_rows = interp.shape[1:3]
    gathered = lax.axis_size("slab") * orient_count * block_rows * images.shape[3] * 2
    pairs = lax.axis_size("slab") == 8
    plan = direct if pairs and gathered <= DIRECT_BYTES else through_owners
    return plan(volume, interp, block_index, images, defocus, orient)


def solution(mesh):
    return jax.shard_map(
        on_device,
        mesh=mesh,
        in_specs=(
            P("slab", None),
            P("img", None, None, "slab"),
            P("img", None, None),
            P("img", "slab", None, None),
            P("img", "slab"),
            P("img", "slab", None),
        ),
        out_specs=(P("slab", None), P("img", "slab", None)),
        check_vma=False,
    )
```

```python
import math

import jax
import jax.numpy as jnp
import numpy as np
from jax import lax
from jax.experimental import pallas as pl
from jax.experimental.pallas import tpu as pltpu
from jax.sharding import PartitionSpec as P

BOX = 256
NS = 16

wave_length = 0.0197
aberration = 27000000.0
amplitude = 0.1
grid_side = 4
LANES = 128
VMEM_LIMIT = 32 << 20
SMEM = pl.BlockSpec(memory_space=pltpu.SMEM)
VMEM = pl.BlockSpec(memory_space=pltpu.VMEM)
DIRECT_BYTES = 4 << 20


def split_bf16(values):
    high = values.astype(jnp.bfloat16)
    low = (values - high.astype(np.float64)).astype(jnp.bfloat16)
    return high, low


def separable_tables(fourier):
    freq = np.arange(fourier) - fourier // 2
    shift = np.arange(NS)
    shift_x = 2 * (shift // grid_side) - (grid_side - 1)
    shift_y = 2 * (shift % grid_side) - (grid_side - 1)
    row = 2.0 * math.pi / BOX * freq[:, None] * shift_x
    col = 2.0 * math.pi / BOX * freq[:, None] * shift_y
    row_table = np.concatenate([np.cos(row), np.sin(row)] * 4, axis=1).astype(np.float32)
    even = np.concatenate([np.cos(col), np.sin(col)], axis=0)
    odd = np.concatenate([-np.sin(col), np.cos(col)], axis=0)
    even_high, even_low = split_bf16(even)
    odd_high, odd_low = split_bf16(odd)
    col_fwd = np.concatenate([even_high, odd_high, even_low, odd_low] * 2, axis=1)
    even = np.concatenate([np.cos(col), -np.sin(col)], axis=0).T
    odd = np.concatenate([-np.sin(col), -np.cos(col)], axis=0).T
    even_high, even_low = split_bf16(even)
    odd_high, odd_low = split_bf16(odd)
    blank = np.zeros((LANES - 4 * NS, 2 * fourier), jnp.bfloat16)
    col_back = np.concatenate([even_high, odd_high, even_low, odd_low, blank], axis=0)
    return row_table, col_fwd, col_back


def sin_turns(turns):
    part = turns - jnp.round(turns)
    folded = jnp.where(part > 0.25, 0.5 - part, jnp.where(part < -0.25, -0.5 - part, part))
    x = folded * (2.0 * math.pi)
    y = x * x
    poly = -1.0 / 39916800.0
    for coefficient in (1.0 / 362880.0, -1.0 / 5040.0, 1.0 / 120.0, -1.0 / 6.0, 1.0):
        poly = poly * y + coefficient
    return x * poly


def weigh_images(images, defocus):
    _, count, fourier, width = images.shape

    def kernel(defocus_ref, image_ref, u_ref):
        kx = lax.broadcasted_iota(jnp.int32, (fourier, fourier), 0) - fourier // 2
        ky = lax.broadcasted_iota(jnp.int32, (fourier, fourier), 1) - fourier // 2
        wave_sq = (kx * kx + ky * ky).astype(jnp.float32) * (1.0 / (BOX * BOX))
        slope = wave_sq * (0.5 * wave_length)
        offset = wave_sq * wave_sq * (-0.25 * aberration * wave_length**3)
        offset = offset + math.asin(amplitude) / (2.0 * math.pi)
        for i in range(count):
            ctf = -sin_turns(defocus_ref[0, i] * slope + offset)
            u_ref[i, :, :fourier] = ctf * image_ref[0, i, :, :fourier].astype(jnp.float32)
            u_ref[i, :, fourier:] = ctf * image_ref[0, i, :, fourier:].astype(jnp.float32)

    return pl.pallas_call(
        kernel,
        out_shape=pltpu.VMEM(images.shape[1:], jnp.float32),
        in_specs=[SMEM, VMEM],
        out_specs=VMEM,
        compiler_params=pltpu.CompilerParams(vmem_limit_bytes=VMEM_LIMIT),
        cost_estimate=pl.CostEstimate(
            flops=30 * count * fourier * fourier, bytes_accessed=6 * count * fourier * width, transcendentals=0
        ),
        name="weigh_images",
    )(defocus, images)


class Reach:
    def __init__(self, me_ref, index_ref, block_rows):
        self.me, self.index, self.block_rows = me_ref[0], index_ref, block_rows

    def __call__(self, j, flip):
        block = self.index[j, jnp.bitwise_xor(self.me, flip)]
        return pl.ds(pl.multiple_of(block * self.block_rows, self.block_rows), self.block_rows)


def add_up_scores(reach, flips, orient_ref, row_ref, fwd_ref, u_ref, part_refs, store):
    count, fourier = u_ref.shape[0], u_ref.shape[1]
    picks = orient_ref.shape[0]
    rows = reach.block_rows
    for i in range(count):
        products, row_parts = [], []
        for k in range(picks):
            j = orient_ref[k, i]
            for flip, part_ref in zip(flips, part_refs):
                where = reach(j, flip)
                real_u = u_ref[i, where, :fourier]
                imag_u = u_ref[i, where, fourier:]
                real_p = part_ref[j, :, :fourier].astype(jnp.float32)
                imag_p = part_ref[j, :, fourier:].astype(jnp.float32)
                products.append(
                    jnp.concatenate(
                        [
                            (real_p * real_u + imag_p * imag_u).astype(jnp.bfloat16),
                            (real_p * imag_u - imag_p * real_u).astype(jnp.bfloat16),
                        ],
                        axis=1,
                    )
                )
                row_parts.append(row_ref[where, :])
        by_row = jnp.dot(jnp.concatenate(products, axis=0), fwd_ref[...], preferred_element_type=jnp.float32)
        for k in range(picks):
            mixed = 0.0
            for s in range(len(flips)):
                at = k * len(flips) + s
                mixed = mixed + by_row[at * rows : (at + 1) * rows] * row_parts[at]
            store(k, i, jnp.sum(mixed, axis=0, keepdims=True))


def add_up_slices(reach, flips, orient_ref, row_ref, back_ref, u_ref, rounded_ref, total):
    count, fourier = u_ref.shape[0], u_ref.shape[1]
    picks = orient_ref.shape[0]
    rows = reach.block_rows
    total[...] = jnp.zeros_like(total)
    for i in range(count):
        mixed = []
        for k in range(picks):
            j = orient_ref[k, i]
            weight = rounded_ref[k, i : i + 1, :]
            for flip in flips:
                mixed.append((row_ref[reach(j, flip), :] * weight).astype(jnp.bfloat16))
        spread = jnp.dot(jnp.concatenate(mixed, axis=0), back_ref[...], preferred_element_type=jnp.float32)
        for k in range(picks):
            j = orient_ref[k, i]
            for s, flip in enumerate(flips):
                where = reach(j, flip)
                at = (k * len(flips) + s) * rows
                real_u = u_ref[i, where, :fourier]
                imag_u = u_ref[i, where, fourier:]
                real_e = spread[at : at + rows, :fourier]
                imag_e = spread[at : at + rows, fourier:]
                total[s, j, :, :fourier] += real_u * real_e - imag_u * imag_e
                total[s, j, :, fourier:] += real_u * imag_e + imag_u * real_e


def first_scores(me, block_index, orient, tables, u, parts, flips):
    count, fourier, width = u.shape
    picks = orient.shape[0]
    block_rows = parts[0].shape[1]

    def kernel(me_ref, index_ref, orient_ref, row_ref, fwd_ref, u_ref, *rest):
        part_refs, score_ref = rest[:-1], rest[-1]
        reach = Reach(me_ref, index_ref, block_rows)

        def store(k, i, value):
            score_ref[k, i : i + 1, :] = value

        add_up_scores(reach, flips, orient_ref, row_ref, fwd_ref, u_ref, part_refs, store)

    return pl.pallas_call(
        kernel,
        out_shape=pltpu.VMEM((picks, count, LANES), jnp.float32),
        in_specs=[SMEM] * 3 + [VMEM] * (3 + len(parts)),
        out_specs=VMEM,
        compiler_params=pltpu.CompilerParams(vmem_limit_bytes=VMEM_LIMIT),
        cost_estimate=pl.CostEstimate(
            flops=len(parts) * count * picks * block_rows * width * LANES * 2,
            bytes_accessed=4 * count * fourier * width,
            transcendentals=0,
        ),
        name="first_scores",
    )(me, block_index, orient, *tables[:2], u, *parts)


def expectation(me, block_index, orient, tables, u, parts, flips, scores, out_flips):
    count, fourier, width = u.shape
    picks = orient.shape[0]
    orient_count, block_rows, _ = parts[0].shape

    def kernel(me_ref, index_ref, orient_ref, row_ref, fwd_ref, back_ref, u_ref, score_ref, *rest):
        part_refs = rest[: len(parts)]
        weights_ref, rounded_ref, rows_ref, total = rest[len(parts) :]
        reach = Reach(me_ref, index_ref, block_rows)

        def store(k, i, value):
            rounded_ref[k, i : i + 1, :] = value

        add_up_scores(reach, flips, orient_ref, row_ref, fwd_ref, u_ref, part_refs, store)
        squared = []
        for k in range(picks):
            value = rounded_ref[k] + score_ref[k]
            value = value + pltpu.roll(value, 2 * NS, 1)
            value = value + pltpu.roll(value, NS, 1)
            value = value * (1.0 / fourier)
            squared.append(value * value)
        mean = jnp.sum(sum(squared), axis=1, keepdims=True) * (1.0 / (LANES * picks))
        scale = 1.0 / (mean + 1e-05)
        lane = lax.broadcasted_iota(jnp.int32, (count, LANES), 1) // NS
        merged = jnp.zeros((count, LANES), jnp.float32)
        for k in range(picks):
            value = squared[k] * scale
            merged = jnp.where(lane == k, value, merged)
            rounded_ref[k] = value.astype(jnp.bfloat16).astype(jnp.float32)
        weights_ref[0] = merged[:, : picks * NS]
        add_up_slices(reach, out_flips, orient_ref, row_ref, back_ref, u_ref, rounded_ref, total)
        rows_ref[...] = total[...].astype(jnp.bfloat16)

    return pl.pallas_call(
        kernel,
        out_shape=(
            pltpu.VMEM((1, count, picks * NS), jnp.float32),
            pltpu.VMEM((picks, count, LANES), jnp.float32),
            pltpu.VMEM((len(out_flips), orient_count, block_rows, width), jnp.bfloat16),
        ),
        in_specs=[SMEM] * 3 + [VMEM] * (5 + len(parts)),
        out_specs=(VMEM,) * 3,
        scratch_shapes=[pltpu.VMEM((len(out_flips), orient_count, block_rows, width), jnp.float32)],
        compiler_params=pltpu.CompilerParams(vmem_limit_bytes=VMEM_LIMIT),
        cost_estimate=pl.CostEstimate(
            flops=(len(parts) + len(out_flips)) * count * picks * block_rows * width * LANES * 2,
            bytes_accessed=4 * count * fourier * width,
            transcendentals=0,
        ),
        name="expectation",
    )(me, block_index, orient, *tables, u, scores, *parts)


def last_slices(me, block_index, orient, tables, u, rounded, block_rows, out_flips):
    count, fourier, width = u.shape
    picks = orient.shape[0]
    orient_count = block_index.shape[0]

    def kernel(me_ref, index_ref, orient_ref, row_ref, back_ref, u_ref, rounded_ref, rows_ref, total):
        reach = Reach(me_ref, index_ref, block_rows)
        add_up_slices(reach, out_flips, orient_ref, row_ref, back_ref, u_ref, rounded_ref, total)
        rows_ref[...] = total[...].astype(jnp.bfloat16)

    return pl.pallas_call(
        kernel,
        out_shape=pltpu.VMEM((len(out_flips), orient_count, block_rows, width), jnp.bfloat16),
        in_specs=[SMEM] * 3 + [VMEM] * 4,
        out_specs=VMEM,
        scratch_shapes=[pltpu.VMEM((len(out_flips), orient_count, block_rows, width), jnp.float32)],
        compiler_params=pltpu.CompilerParams(vmem_limit_bytes=VMEM_LIMIT),
        cost_estimate=pl.CostEstimate(
            flops=len(out_flips) * count * picks * block_rows * width * LANES * 2,
            bytes_accessed=4 * count * fourier * width,
            transcendentals=0,
        ),
        name="last_slices",
    )(me, block_index, orient, tables[0], tables[2], u, rounded)


def swap(value, axis, size, flip):
    return lax.ppermute(value, axis, [(source, source ^ flip) for source in range(size)])


def together(*values):
    return sum(value.astype(jnp.float32) for value in values).astype(jnp.bfloat16)


def direct(volume, interp, block_index, images, defocus, orient):
    slab_count = lax.axis_size("slab")
    group_count = lax.axis_size("img")
    orient_count, block_rows, slab_rows = interp.shape[1:]
    fourier, width = images.shape[2:]
    image_count = images.shape[1] * slab_count
    near, far, other, side = 2, 4, 6, 1

    def to(value, flip):
        return swap(value, "slab", slab_count, flip)

    weigher = interp[0].reshape(orient_count * block_rows, slab_rows)
    own = jnp.dot(weigher, volume, preferred_element_type=jnp.float32).astype(jnp.bfloat16)
    own = own.reshape(orient_count, block_rows, width)
    from_other, from_far, from_near, from_side = (to(own, flip) for flip in (other, far, near, side))
    from_near_side = to(from_near, side)
    u = weigh_images(images, defocus)
    from_far, u = lax.optimization_barrier((from_far, u))
    from_other, _ = lax.optimization_barrier((from_other, from_far))
    from_far_side, from_other_side = to(from_far, side), to(from_other, side)

    common = lax.axis_index("slab").astype(jnp.int32).reshape(1), block_index[0], orient[0].T, separable_tables(fourier), u
    scores = first_scores(*common, [own, from_near, from_far, from_other, from_side, from_near_side], (0, near, far, other, side, near + side))
    late_weigher, scores = lax.optimization_barrier((weigher, scores))
    weigher_across = swap(late_weigher, "img", group_count, 2)
    weights, rounded, side_rows = expectation(
        *common,
        [from_far_side, from_other_side],
        (far + side, other + side),
        scores,
        (other + side, far + side, near + side, side),
    )
    first = to(side_rows[0], side)
    rest = to(side_rows[1:], side)
    weigher_across, rounded = lax.optimization_barrier((weigher_across, rounded))
    rows = last_slices(*common, rounded, block_rows, (other, far, near, 0))
    back = together(
        rows[3],
        rest[2],
        to(together(rows[0], first), other),
        to(together(rows[1], rest[0]), far),
        to(together(rows[2], rest[1]), near),
    ).reshape(orient_count * block_rows, width)

    def all_groups(value):
        across = swap(value, "img", group_count, 2)
        return [value, swap(value, "img", group_count, 1), across, swap(across, "img", group_count, 1)]

    weighers = [weigher, swap(weigher, "img", group_count, 1), weigher_across, swap(weigher_across, "img", group_count, 1)]
    backs = all_groups(back)
    update = lax.dot_general(
        jnp.concatenate(weighers, axis=0),
        jnp.concatenate(backs, axis=0),
        (((0,), (0,)), ((), ())),
        preferred_element_type=jnp.float32,
    )
    return update / math.sqrt(image_count), weights


def phase_tables(fourier, shifts, box):
    freq = (jnp.arange(fourier, dtype=jnp.int32) - fourier // 2).astype(jnp.float32)
    shift_steps = jnp.arange(shifts, dtype=jnp.int32)
    shift_x = (2 * (shift_steps // grid_side) - (grid_side - 1)).astype(jnp.float32)
    shift_y = (2 * (shift_steps % grid_side) - (grid_side - 1)).astype(jnp.float32)
    angle = 2.0 * math.pi / box * (freq[:, None, None] * shift_x + freq[None, :, None] * shift_y)
    forward = jnp.stack([jnp.cos(angle), jnp.sin(angle)], axis=1).reshape(
        2 * fourier * fourier, shifts
    )
    backward = jnp.stack([jnp.cos(angle), -jnp.sin(angle)], axis=1).reshape(
        2 * fourier * fourier, shifts
    )
    return (forward.astype(jnp.bfloat16), backward.T.astype(jnp.bfloat16))


def contrast(defocus_blk, fourier, box):
    freq = (jnp.arange(fourier, dtype=jnp.int32) - fourier // 2).astype(jnp.float32)
    wave_sq = (freq[:, None] * freq[:, None] + freq[None, :] * freq[None, :]) / (box * box)
    phase = math.pi * wave_length * defocus_blk[:, None, None] * wave_sq
    phase = phase - 0.5 * math.pi * aberration * wave_length**3 * wave_sq * wave_sq
    return -(math.sqrt(1.0 - amplitude * amplitude) * jnp.sin(phase) + amplitude * jnp.cos(phase))


def correlate(panels, image_blk, list_blk, defocus_blk, phase_fwd, phase_back, box):
    count = image_blk.shape[0]
    fourier = image_blk.shape[1]
    picks = list_blk.shape[1]
    shifts = phase_fwd.shape[1]
    ctf = contrast(defocus_blk, fourier, box)
    weighted = ctf[:, :, None, :] * image_blk.astype(jnp.float32).reshape(
        count, fourier, 2, fourier
    )
    real_u = weighted[:, None, :, 0]
    imag_u = weighted[:, None, :, 1]
    chosen = panels[list_blk].astype(jnp.float32).reshape(count, picks, fourier, 2, fourier)
    real_p = chosen[:, :, :, 0]
    imag_p = chosen[:, :, :, 1]
    product = jnp.stack(
        [real_p * real_u + imag_p * imag_u, real_p * imag_u - imag_p * real_u], axis=3
    )
    product = product.astype(jnp.bfloat16).reshape(count * picks, 2 * fourier * fourier)
    scores = jnp.dot(product, phase_fwd, preferred_element_type=jnp.float32) / fourier
    scores = scores.reshape(count, picks * shifts)
    squared = scores * scores
    weights = squared / (jnp.mean(squared, axis=1, keepdims=True) + 1e-05)
    rounded = weights.astype(jnp.bfloat16).reshape(count * picks, shifts)
    spread = jnp.dot(rounded, phase_back, preferred_element_type=jnp.float32)
    spread = spread.reshape(count, picks, fourier, 2, fourier)
    real_e = spread[:, :, :, 0]
    imag_e = spread[:, :, :, 1]
    backed = jnp.stack(
        [real_u * real_e - imag_u * imag_e, real_u * imag_e + imag_u * real_e], axis=3
    )
    backed = backed.astype(jnp.bfloat16).reshape(count * picks, 2 * fourier * fourier)
    return (weights, backed)


def through_owners(volume, interp, block_index, images, defocus, orient):
    slab_count = lax.axis_size("slab")
    slab_index = lax.axis_index("slab")
    orient_count = interp.shape[1]
    ori_dev = orient_count // slab_count
    block_rows = interp.shape[2]
    fourier = images.shape[2]
    block_count = fourier // block_rows
    img_dev = images.shape[1]
    picks = orient.shape[2]
    levels = jnp.arange(block_count, dtype=jnp.int32)
    partial_value = jnp.einsum("jpr,rx->jpx", interp[0], volume, preferred_element_type=jnp.float32)
    owned_idx = lax.dynamic_slice_in_dim(block_index[0], slab_index * ori_dev, ori_dev, 0)
    arrived = lax.all_to_all(partial_value, "slab", split_axis=0, concat_axis=0, tiled=True)
    arrived = arrived.reshape(slab_count, ori_dev, block_rows, 2 * fourier)
    chosen = (owned_idx[:, :, None] == levels).astype(jnp.float32)
    summed = jnp.einsum("osb,sopx->obpx", chosen, arrived, precision=lax.Precision.HIGHEST)
    summed = summed.reshape(ori_dev, fourier, 2 * fourier)
    panels = lax.all_gather(summed.astype(jnp.bfloat16), "slab", axis=0, tiled=True)
    phase_fwd, phase_back = phase_tables(fourier, NS, BOX)
    blk = math.gcd(img_dev, 32)
    blk_total = img_dev // blk

    def per_block(pieces):
        image_blk, list_blk, defocus_blk = pieces
        return correlate(panels, image_blk, list_blk, defocus_blk, phase_fwd, phase_back, BOX)

    weights, backs = lax.map(
        per_block,
        (
            images[0].reshape(blk_total, blk, fourier, 2 * fourier),
            orient[0].reshape(blk_total, blk, picks),
            defocus[0].reshape(blk_total, blk),
        ),
    )
    all_slices = backs.reshape(img_dev * picks, 2 * fourier * fourier)
    member = (
        orient[0].reshape(-1)[:, None] == jnp.arange(orient_count, dtype=jnp.int32)[None, :]
    ).astype(jnp.bfloat16)
    back_own = lax.psum_scatter(
        lax.dot_general(
            member, all_slices, (((0,), (0,)), ((), ())), preferred_element_type=jnp.float32
        ),
        "slab",
        scatter_dimension=0,
        tiled=True,
    ).astype(jnp.bfloat16)
    back_own = back_own.reshape(ori_dev, block_count, block_rows, 2 * fourier)
    chosen_back = (owned_idx[:, :, None] == levels).astype(jnp.bfloat16)
    outgoing = jnp.einsum(
        "osb,obpx->sopx", chosen_back, back_own, preferred_element_type=jnp.float32
    )
    outgoing = outgoing.astype(jnp.bfloat16).reshape(slab_count * ori_dev, block_rows, 2 * fourier)
    incoming = lax.all_to_all(outgoing, "slab", split_axis=0, concat_axis=0, tiled=True)
    column = jnp.einsum("jpr,jpx->rx", interp[0], incoming, preferred_element_type=jnp.float32)
    summed_cols = lax.psum(column, "img")
    update = summed_cols / math.sqrt(img_dev * slab_count)
    return (update, weights)


def on_device(volume, interp, block_index, images, defocus, orient):
    orient_count, block_rows = interp.shape[1:3]
    gathered = lax.axis_size("slab") * orient_count * block_rows * images.shape[3] * 2
    pairs = lax.axis_size("slab") == 8 and lax.axis_size("img") == 4
    plan = direct if pairs and gathered <= DIRECT_BYTES else through_owners
    return plan(volume, interp, block_index, images, defocus, orient)


def solution(mesh):
    return jax.shard_map(
        on_device,
        mesh=mesh,
        in_specs=(
            P("slab", None),
            P("img", None, None, "slab"),
            P("img", None, None),
            P("img", "slab", None, None),
            P("img", "slab"),
            P("img", "slab", None),
        ),
        out_specs=(P("slab", None), P("img", "slab", None)),
        check_vma=False,
    )
```

```python
import math

import jax
import jax.numpy as jnp
import numpy as np
from jax import lax
from jax.experimental import pallas as pl
from jax.experimental.pallas import tpu as pltpu
from jax.sharding import PartitionSpec as P

BOX = 256
NS = 16

wave_length = 0.0197
aberration = 27000000.0
amplitude = 0.1
grid_side = 4
LANES = 128
VMEM_LIMIT = 32 << 20
SMEM = pl.BlockSpec(memory_space=pltpu.SMEM)
VMEM = pl.BlockSpec(memory_space=pltpu.VMEM)
DIRECT_BYTES = 4 << 20


def split_bf16(values):
    high = values.astype(jnp.bfloat16)
    low = (values - high.astype(np.float64)).astype(jnp.bfloat16)
    return high, low


def separable_tables(fourier):
    freq = np.arange(fourier) - fourier // 2
    shift = np.arange(NS)
    shift_x = 2 * (shift // grid_side) - (grid_side - 1)
    shift_y = 2 * (shift % grid_side) - (grid_side - 1)
    row = 2.0 * math.pi / BOX * freq[:, None] * shift_x
    col = 2.0 * math.pi / BOX * freq[:, None] * shift_y
    row_table = np.concatenate([np.cos(row), np.sin(row)] * 4, axis=1).astype(np.float32)
    even = np.concatenate([np.cos(col), np.sin(col)], axis=0)
    odd = np.concatenate([-np.sin(col), np.cos(col)], axis=0)
    even_high, even_low = split_bf16(even)
    odd_high, odd_low = split_bf16(odd)
    col_fwd = np.concatenate([even_high, odd_high, even_low, odd_low] * 2, axis=1)
    even = np.concatenate([np.cos(col), -np.sin(col)], axis=0).T
    odd = np.concatenate([-np.sin(col), -np.cos(col)], axis=0).T
    even_high, even_low = split_bf16(even)
    odd_high, odd_low = split_bf16(odd)
    blank = np.zeros((LANES - 4 * NS, 2 * fourier), jnp.bfloat16)
    col_back = np.concatenate([even_high, odd_high, even_low, odd_low, blank], axis=0)
    return row_table, col_fwd, col_back


def sin_turns(turns):
    part = turns - jnp.round(turns)
    folded = jnp.where(part > 0.25, 0.5 - part, jnp.where(part < -0.25, -0.5 - part, part))
    x = folded * (2.0 * math.pi)
    y = x * x
    poly = -1.0 / 39916800.0
    for coefficient in (1.0 / 362880.0, -1.0 / 5040.0, 1.0 / 120.0, -1.0 / 6.0, 1.0):
        poly = poly * y + coefficient
    return x * poly


def weigh_images(images, defocus):
    _, count, fourier, width = images.shape

    def kernel(defocus_ref, image_ref, u_ref):
        kx = lax.broadcasted_iota(jnp.int32, (fourier, fourier), 0) - fourier // 2
        ky = lax.broadcasted_iota(jnp.int32, (fourier, fourier), 1) - fourier // 2
        wave_sq = (kx * kx + ky * ky).astype(jnp.float32) * (1.0 / (BOX * BOX))
        slope = wave_sq * (0.5 * wave_length)
        offset = wave_sq * wave_sq * (-0.25 * aberration * wave_length**3)
        offset = offset + math.asin(amplitude) / (2.0 * math.pi)
        for i in range(count):
            ctf = -sin_turns(defocus_ref[0, i] * slope + offset)
            u_ref[i, :, :fourier] = ctf * image_ref[0, i, :, :fourier].astype(jnp.float32)
            u_ref[i, :, fourier:] = ctf * image_ref[0, i, :, fourier:].astype(jnp.float32)

    return pl.pallas_call(
        kernel,
        out_shape=pltpu.VMEM(images.shape[1:], jnp.float32),
        in_specs=[SMEM, VMEM],
        out_specs=VMEM,
        compiler_params=pltpu.CompilerParams(vmem_limit_bytes=VMEM_LIMIT),
        cost_estimate=pl.CostEstimate(
            flops=30 * count * fourier * fourier, bytes_accessed=6 * count * fourier * width, transcendentals=0
        ),
        name="weigh_images",
    )(defocus, images)


class Reach:
    def __init__(self, me_ref, index_ref, block_rows):
        self.me, self.index, self.block_rows = me_ref[0], index_ref, block_rows

    def __call__(self, j, flip):
        block = self.index[j, jnp.bitwise_xor(self.me, flip)]
        return pl.ds(pl.multiple_of(block * self.block_rows, self.block_rows), self.block_rows)


def add_up_scores(reach, flips, orient_ref, row_ref, fwd_ref, u_ref, part_refs, store):
    count, fourier = u_ref.shape[0], u_ref.shape[1]
    picks = orient_ref.shape[0]
    rows = reach.block_rows
    for i in range(count):
        products, row_parts = [], []
        for k in range(picks):
            j = orient_ref[k, i]
            for flip, part_ref in zip(flips, part_refs):
                where = reach(j, flip)
                real_u = u_ref[i, where, :fourier]
                imag_u = u_ref[i, where, fourier:]
                real_p = part_ref[j, :, :fourier].astype(jnp.float32)
                imag_p = part_ref[j, :, fourier:].astype(jnp.float32)
                products.append(
                    jnp.concatenate(
                        [
                            (real_p * real_u + imag_p * imag_u).astype(jnp.bfloat16),
                            (real_p * imag_u - imag_p * real_u).astype(jnp.bfloat16),
                        ],
                        axis=1,
                    )
                )
                row_parts.append(row_ref[where, :])
        by_row = jnp.dot(jnp.concatenate(products, axis=0), fwd_ref[...], preferred_element_type=jnp.float32)
        for k in range(picks):
            mixed = 0.0
            for s in range(len(flips)):
                at = k * len(flips) + s
                mixed = mixed + by_row[at * rows : (at + 1) * rows] * row_parts[at]
            store(k, i, jnp.sum(mixed, axis=0, keepdims=True))


def add_up_slices(reach, flips, orient_ref, row_ref, back_ref, u_ref, rounded_ref, total):
    count, fourier = u_ref.shape[0], u_ref.shape[1]
    picks = orient_ref.shape[0]
    rows = reach.block_rows
    total[...] = jnp.zeros_like(total)
    for i in range(count):
        mixed = []
        for k in range(picks):
            j = orient_ref[k, i]
            weight = rounded_ref[k, i : i + 1, :]
            for flip in flips:
                mixed.append((row_ref[reach(j, flip), :] * weight).astype(jnp.bfloat16))
        spread = jnp.dot(jnp.concatenate(mixed, axis=0), back_ref[...], preferred_element_type=jnp.float32)
        for k in range(picks):
            j = orient_ref[k, i]
            for s, flip in enumerate(flips):
                where = reach(j, flip)
                at = (k * len(flips) + s) * rows
                real_u = u_ref[i, where, :fourier]
                imag_u = u_ref[i, where, fourier:]
                real_e = spread[at : at + rows, :fourier]
                imag_e = spread[at : at + rows, fourier:]
                total[s, j, :, :fourier] += real_u * real_e - imag_u * imag_e
                total[s, j, :, fourier:] += real_u * imag_e + imag_u * real_e


def first_scores(me, block_index, orient, tables, u, parts, flips):
    count, fourier, width = u.shape
    picks = orient.shape[0]
    block_rows = parts[0].shape[1]

    def kernel(me_ref, index_ref, orient_ref, row_ref, fwd_ref, u_ref, *rest):
        part_refs, score_ref = rest[:-1], rest[-1]
        reach = Reach(me_ref, index_ref, block_rows)

        def store(k, i, value):
            score_ref[k, i : i + 1, :] = value

        add_up_scores(reach, flips, orient_ref, row_ref, fwd_ref, u_ref, part_refs, store)

    return pl.pallas_call(
        kernel,
        out_shape=pltpu.VMEM((picks, count, LANES), jnp.float32),
        in_specs=[SMEM] * 3 + [VMEM] * (3 + len(parts)),
        out_specs=VMEM,
        compiler_params=pltpu.CompilerParams(vmem_limit_bytes=VMEM_LIMIT),
        cost_estimate=pl.CostEstimate(
            flops=len(parts) * count * picks * block_rows * width * LANES * 2,
            bytes_accessed=4 * count * fourier * width,
            transcendentals=0,
        ),
        name="first_scores",
    )(me, block_index, orient, *tables[:2], u, *parts)


def expectation(me, block_index, orient, tables, u, parts, flips, scores, out_flips):
    count, fourier, width = u.shape
    picks = orient.shape[0]
    orient_count, block_rows, _ = parts[0].shape

    def kernel(me_ref, index_ref, orient_ref, row_ref, fwd_ref, back_ref, u_ref, score_ref, *rest):
        part_refs = rest[: len(parts)]
        weights_ref, rounded_ref, rows_ref, total = rest[len(parts) :]
        reach = Reach(me_ref, index_ref, block_rows)

        def store(k, i, value):
            rounded_ref[k, i : i + 1, :] = value

        add_up_scores(reach, flips, orient_ref, row_ref, fwd_ref, u_ref, part_refs, store)
        squared = []
        for k in range(picks):
            value = rounded_ref[k] + score_ref[k]
            value = value + pltpu.roll(value, 2 * NS, 1)
            value = value + pltpu.roll(value, NS, 1)
            value = value * (1.0 / fourier)
            squared.append(value * value)
        mean = jnp.sum(sum(squared), axis=1, keepdims=True) * (1.0 / (LANES * picks))
        scale = 1.0 / (mean + 1e-05)
        lane = lax.broadcasted_iota(jnp.int32, (count, LANES), 1) // NS
        merged = jnp.zeros((count, LANES), jnp.float32)
        for k in range(picks):
            value = squared[k] * scale
            merged = jnp.where(lane == k, value, merged)
            rounded_ref[k] = value.astype(jnp.bfloat16).astype(jnp.float32)
        weights_ref[0] = merged[:, : picks * NS]
        add_up_slices(reach, out_flips, orient_ref, row_ref, back_ref, u_ref, rounded_ref, total)
        rows_ref[...] = total[...].astype(jnp.bfloat16)

    return pl.pallas_call(
        kernel,
        out_shape=(
            pltpu.VMEM((1, count, picks * NS), jnp.float32),
            pltpu.VMEM((picks, count, LANES), jnp.float32),
            pltpu.VMEM((len(out_flips), orient_count, block_rows, width), jnp.bfloat16),
        ),
        in_specs=[SMEM] * 3 + [VMEM] * (5 + len(parts)),
        out_specs=(VMEM,) * 3,
        scratch_shapes=[pltpu.VMEM((len(out_flips), orient_count, block_rows, width), jnp.float32)],
        compiler_params=pltpu.CompilerParams(vmem_limit_bytes=VMEM_LIMIT),
        cost_estimate=pl.CostEstimate(
            flops=(len(parts) + len(out_flips)) * count * picks * block_rows * width * LANES * 2,
            bytes_accessed=4 * count * fourier * width,
            transcendentals=0,
        ),
        name="expectation",
    )(me, block_index, orient, *tables, u, scores, *parts)


def last_slices(me, block_index, orient, tables, u, rounded, block_rows, out_flips):
    count, fourier, width = u.shape
    picks = orient.shape[0]
    orient_count = block_index.shape[0]

    def kernel(me_ref, index_ref, orient_ref, row_ref, back_ref, u_ref, rounded_ref, rows_ref, total):
        reach = Reach(me_ref, index_ref, block_rows)
        add_up_slices(reach, out_flips, orient_ref, row_ref, back_ref, u_ref, rounded_ref, total)
        rows_ref[...] = total[...].astype(jnp.bfloat16)

    return pl.pallas_call(
        kernel,
        out_shape=pltpu.VMEM((len(out_flips), orient_count, block_rows, width), jnp.bfloat16),
        in_specs=[SMEM] * 3 + [VMEM] * 4,
        out_specs=VMEM,
        scratch_shapes=[pltpu.VMEM((len(out_flips), orient_count, block_rows, width), jnp.float32)],
        compiler_params=pltpu.CompilerParams(vmem_limit_bytes=VMEM_LIMIT),
        cost_estimate=pl.CostEstimate(
            flops=len(out_flips) * count * picks * block_rows * width * LANES * 2,
            bytes_accessed=4 * count * fourier * width,
            transcendentals=0,
        ),
        name="last_slices",
    )(me, block_index, orient, tables[0], tables[2], u, rounded)


def swap(value, axis, size, flip):
    return lax.ppermute(value, axis, [(source, source ^ flip) for source in range(size)])


def together(*values):
    return sum(value.astype(jnp.float32) for value in values).astype(jnp.bfloat16)


def direct(volume, interp, block_index, images, defocus, orient):
    slab_count = lax.axis_size("slab")
    group_count = lax.axis_size("img")
    orient_count, block_rows, slab_rows = interp.shape[1:]
    fourier, width = images.shape[2:]
    image_count = images.shape[1] * slab_count
    near, far, other, side = 2, 4, 6, 1

    def to(value, flip):
        return swap(value, "slab", slab_count, flip)

    weigher = interp[0].reshape(orient_count * block_rows, slab_rows)
    own = jnp.dot(weigher, volume, preferred_element_type=jnp.float32).astype(jnp.bfloat16)
    own = own.reshape(orient_count, block_rows, width)
    from_other, from_far, from_near, from_side = (to(own, flip) for flip in (other, far, near, side))
    from_near_side = to(from_near, side)
    u = weigh_images(images, defocus)
    from_far, from_other, u, from_side, from_near_side = lax.optimization_barrier((from_far, from_other, u, from_side, from_near_side))
    from_far_side, from_other_side = to(jnp.stack([from_far, from_other]), side)

    common = lax.axis_index("slab").astype(jnp.int32).reshape(1), block_index[0], orient[0].T, separable_tables(fourier), u
    scores = first_scores(*common, [own, from_near, from_far, from_other, from_side, from_near_side], (0, near, far, other, side, near + side))
    late_weigher, scores = lax.optimization_barrier((weigher, scores))
    weigher_across = swap(late_weigher, "img", group_count, 2)
    weights, rounded, side_rows = expectation(
        *common,
        [from_far_side, from_other_side],
        (far + side, other + side),
        scores,
        (other + side, far + side, near + side, side),
    )
    first = to(side_rows[0], side)
    rest = to(side_rows[1:], side)
    weigher_across, rounded = lax.optimization_barrier((weigher_across, rounded))
    rows = last_slices(*common, rounded, block_rows, (other, far, near, 0))
    back = together(
        rows[3],
        rest[2],
        to(together(rows[0], first), other),
        to(together(rows[1], rest[0]), far),
        to(together(rows[2], rest[1]), near),
    ).reshape(orient_count * block_rows, width)

    def all_groups(value):
        across = swap(value, "img", group_count, 2)
        return [value, swap(value, "img", group_count, 1), across, swap(across, "img", group_count, 1)]

    weighers = [weigher, swap(weigher, "img", group_count, 1), weigher_across, swap(weigher_across, "img", group_count, 1)]
    backs = all_groups(back)
    update = lax.dot_general(
        jnp.concatenate(weighers, axis=0),
        jnp.concatenate(backs, axis=0),
        (((0,), (0,)), ((), ())),
        preferred_element_type=jnp.float32,
    )
    return update / math.sqrt(image_count), weights


def phase_tables(fourier, shifts, box):
    freq = (jnp.arange(fourier, dtype=jnp.int32) - fourier // 2).astype(jnp.float32)
    shift_steps = jnp.arange(shifts, dtype=jnp.int32)
    shift_x = (2 * (shift_steps // grid_side) - (grid_side - 1)).astype(jnp.float32)
    shift_y = (2 * (shift_steps % grid_side) - (grid_side - 1)).astype(jnp.float32)
    angle = 2.0 * math.pi / box * (freq[:, None, None] * shift_x + freq[None, :, None] * shift_y)
    forward = jnp.stack([jnp.cos(angle), jnp.sin(angle)], axis=1).reshape(
        2 * fourier * fourier, shifts
    )
    backward = jnp.stack([jnp.cos(angle), -jnp.sin(angle)], axis=1).reshape(
        2 * fourier * fourier, shifts
    )
    return (forward.astype(jnp.bfloat16), backward.T.astype(jnp.bfloat16))


def contrast(defocus_blk, fourier, box):
    freq = (jnp.arange(fourier, dtype=jnp.int32) - fourier // 2).astype(jnp.float32)
    wave_sq = (freq[:, None] * freq[:, None] + freq[None, :] * freq[None, :]) / (box * box)
    phase = math.pi * wave_length * defocus_blk[:, None, None] * wave_sq
    phase = phase - 0.5 * math.pi * aberration * wave_length**3 * wave_sq * wave_sq
    return -(math.sqrt(1.0 - amplitude * amplitude) * jnp.sin(phase) + amplitude * jnp.cos(phase))


def correlate(panels, image_blk, list_blk, defocus_blk, phase_fwd, phase_back, box):
    count = image_blk.shape[0]
    fourier = image_blk.shape[1]
    picks = list_blk.shape[1]
    shifts = phase_fwd.shape[1]
    ctf = contrast(defocus_blk, fourier, box)
    weighted = ctf[:, :, None, :] * image_blk.astype(jnp.float32).reshape(
        count, fourier, 2, fourier
    )
    real_u = weighted[:, None, :, 0]
    imag_u = weighted[:, None, :, 1]
    chosen = panels[list_blk].astype(jnp.float32).reshape(count, picks, fourier, 2, fourier)
    real_p = chosen[:, :, :, 0]
    imag_p = chosen[:, :, :, 1]
    product = jnp.stack(
        [real_p * real_u + imag_p * imag_u, real_p * imag_u - imag_p * real_u], axis=3
    )
    product = product.astype(jnp.bfloat16).reshape(count * picks, 2 * fourier * fourier)
    scores = jnp.dot(product, phase_fwd, preferred_element_type=jnp.float32) / fourier
    scores = scores.reshape(count, picks * shifts)
    squared = scores * scores
    weights = squared / (jnp.mean(squared, axis=1, keepdims=True) + 1e-05)
    rounded = weights.astype(jnp.bfloat16).reshape(count * picks, shifts)
    spread = jnp.dot(rounded, phase_back, preferred_element_type=jnp.float32)
    spread = spread.reshape(count, picks, fourier, 2, fourier)
    real_e = spread[:, :, :, 0]
    imag_e = spread[:, :, :, 1]
    backed = jnp.stack(
        [real_u * real_e - imag_u * imag_e, real_u * imag_e + imag_u * real_e], axis=3
    )
    backed = backed.astype(jnp.bfloat16).reshape(count * picks, 2 * fourier * fourier)
    return (weights, backed)


def through_owners(volume, interp, block_index, images, defocus, orient):
    slab_count = lax.axis_size("slab")
    slab_index = lax.axis_index("slab")
    orient_count = interp.shape[1]
    ori_dev = orient_count // slab_count
    block_rows = interp.shape[2]
    fourier = images.shape[2]
    block_count = fourier // block_rows
    img_dev = images.shape[1]
    picks = orient.shape[2]
    levels = jnp.arange(block_count, dtype=jnp.int32)
    partial_value = jnp.einsum("jpr,rx->jpx", interp[0], volume, preferred_element_type=jnp.float32)
    owned_idx = lax.dynamic_slice_in_dim(block_index[0], slab_index * ori_dev, ori_dev, 0)
    arrived = lax.all_to_all(partial_value, "slab", split_axis=0, concat_axis=0, tiled=True)
    arrived = arrived.reshape(slab_count, ori_dev, block_rows, 2 * fourier)
    chosen = (owned_idx[:, :, None] == levels).astype(jnp.float32)
    summed = jnp.einsum("osb,sopx->obpx", chosen, arrived, precision=lax.Precision.HIGHEST)
    summed = summed.reshape(ori_dev, fourier, 2 * fourier)
    panels = lax.all_gather(summed.astype(jnp.bfloat16), "slab", axis=0, tiled=True)
    phase_fwd, phase_back = phase_tables(fourier, NS, BOX)
    blk = math.gcd(img_dev, 32)
    blk_total = img_dev // blk

    def per_block(pieces):
        image_blk, list_blk, defocus_blk = pieces
        return correlate(panels, image_blk, list_blk, defocus_blk, phase_fwd, phase_back, BOX)

    weights, backs = lax.map(
        per_block,
        (
            images[0].reshape(blk_total, blk, fourier, 2 * fourier),
            orient[0].reshape(blk_total, blk, picks),
            defocus[0].reshape(blk_total, blk),
        ),
    )
    all_slices = backs.reshape(img_dev * picks, 2 * fourier * fourier)
    member = (
        orient[0].reshape(-1)[:, None] == jnp.arange(orient_count, dtype=jnp.int32)[None, :]
    ).astype(jnp.bfloat16)
    back_own = lax.psum_scatter(
        lax.dot_general(
            member, all_slices, (((0,), (0,)), ((), ())), preferred_element_type=jnp.float32
        ),
        "slab",
        scatter_dimension=0,
        tiled=True,
    ).astype(jnp.bfloat16)
    back_own = back_own.reshape(ori_dev, block_count, block_rows, 2 * fourier)
    chosen_back = (owned_idx[:, :, None] == levels).astype(jnp.bfloat16)
    outgoing = jnp.einsum(
        "osb,obpx->sopx", chosen_back, back_own, preferred_element_type=jnp.float32
    )
    outgoing = outgoing.astype(jnp.bfloat16).reshape(slab_count * ori_dev, block_rows, 2 * fourier)
    incoming = lax.all_to_all(outgoing, "slab", split_axis=0, concat_axis=0, tiled=True)
    column = jnp.einsum("jpr,jpx->rx", interp[0], incoming, preferred_element_type=jnp.float32)
    summed_cols = lax.psum(column, "img")
    update = summed_cols / math.sqrt(img_dev * slab_count)
    return (update, weights)


def on_device(volume, interp, block_index, images, defocus, orient):
    orient_count, block_rows = interp.shape[1:3]
    gathered = lax.axis_size("slab") * orient_count * block_rows * images.shape[3] * 2
    pairs = lax.axis_size("slab") == 8 and lax.axis_size("img") == 4
    plan = direct if pairs and gathered <= DIRECT_BYTES else through_owners
    return plan(volume, interp, block_index, images, defocus, orient)


def solution(mesh):
    return jax.shard_map(
        on_device,
        mesh=mesh,
        in_specs=(
            P("slab", None),
            P("img", None, None, "slab"),
            P("img", None, None),
            P("img", "slab", None, None),
            P("img", "slab"),
            P("img", "slab", None),
        ),
        out_specs=(P("slab", None), P("img", "slab", None)),
        check_vma=False,
    )
```

```python
import math

import jax
import jax.numpy as jnp
import numpy as np
from jax import lax
from jax.experimental import pallas as pl
from jax.experimental.pallas import tpu as pltpu
from jax.sharding import PartitionSpec as P

BOX = 256
NS = 16

wave_length = 0.0197
aberration = 27000000.0
amplitude = 0.1
grid_side = 4
LANES = 128
VMEM_LIMIT = 32 << 20
SMEM = pl.BlockSpec(memory_space=pltpu.SMEM)
VMEM = pl.BlockSpec(memory_space=pltpu.VMEM)
DIRECT_BYTES = 4 << 20


def split_bf16(values):
    high = values.astype(jnp.bfloat16)
    low = (values - high.astype(np.float64)).astype(jnp.bfloat16)
    return high, low


def separable_tables(fourier):
    freq = np.arange(fourier) - fourier // 2
    shift = np.arange(NS)
    shift_x = 2 * (shift // grid_side) - (grid_side - 1)
    shift_y = 2 * (shift % grid_side) - (grid_side - 1)
    row = 2.0 * math.pi / BOX * freq[:, None] * shift_x
    col = 2.0 * math.pi / BOX * freq[:, None] * shift_y
    row_table = np.concatenate([np.cos(row), np.sin(row)] * 4, axis=1).astype(np.float32)
    even = np.concatenate([np.cos(col), np.sin(col)], axis=0)
    odd = np.concatenate([-np.sin(col), np.cos(col)], axis=0)
    even_high, even_low = split_bf16(even)
    odd_high, odd_low = split_bf16(odd)
    col_fwd = np.concatenate([even_high, odd_high, even_low, odd_low] * 2, axis=1)
    even = np.concatenate([np.cos(col), -np.sin(col)], axis=0).T
    odd = np.concatenate([-np.sin(col), -np.cos(col)], axis=0).T
    even_high, even_low = split_bf16(even)
    odd_high, odd_low = split_bf16(odd)
    blank = np.zeros((LANES - 4 * NS, 2 * fourier), jnp.bfloat16)
    col_back = np.concatenate([even_high, odd_high, even_low, odd_low, blank], axis=0)
    return row_table, col_fwd, col_back


def sin_turns(turns):
    part = turns - jnp.round(turns)
    folded = jnp.where(part > 0.25, 0.5 - part, jnp.where(part < -0.25, -0.5 - part, part))
    x = folded * (2.0 * math.pi)
    y = x * x
    poly = -1.0 / 39916800.0
    for coefficient in (1.0 / 362880.0, -1.0 / 5040.0, 1.0 / 120.0, -1.0 / 6.0, 1.0):
        poly = poly * y + coefficient
    return x * poly


def weigh_images(images, defocus):
    _, count, fourier, width = images.shape

    def kernel(defocus_ref, image_ref, u_ref):
        kx = lax.broadcasted_iota(jnp.int32, (fourier, fourier), 0) - fourier // 2
        ky = lax.broadcasted_iota(jnp.int32, (fourier, fourier), 1) - fourier // 2
        wave_sq = (kx * kx + ky * ky).astype(jnp.float32) * (1.0 / (BOX * BOX))
        slope = wave_sq * (0.5 * wave_length)
        offset = wave_sq * wave_sq * (-0.25 * aberration * wave_length**3)
        offset = offset + math.asin(amplitude) / (2.0 * math.pi)
        for i in range(count):
            ctf = -sin_turns(defocus_ref[0, i] * slope + offset)
            u_ref[i, :, :fourier] = ctf * image_ref[0, i, :, :fourier].astype(jnp.float32)
            u_ref[i, :, fourier:] = ctf * image_ref[0, i, :, fourier:].astype(jnp.float32)

    return pl.pallas_call(
        kernel,
        out_shape=pltpu.VMEM(images.shape[1:], jnp.float32),
        in_specs=[SMEM, VMEM],
        out_specs=VMEM,
        compiler_params=pltpu.CompilerParams(vmem_limit_bytes=VMEM_LIMIT),
        cost_estimate=pl.CostEstimate(
            flops=30 * count * fourier * fourier, bytes_accessed=6 * count * fourier * width, transcendentals=0
        ),
        name="weigh_images",
    )(defocus, images)


class Places:
    def __init__(self, first_ref, orient_ref, block_rows):
        self.first_ref, self.orient_ref, self.block_rows = first_ref, orient_ref, block_rows
        self.picks = orient_ref.shape[0]

    def rows(self, i, k, flip):
        first = self.first_ref[self.orient_ref[k, i], flip]
        return pl.ds(pl.multiple_of(first, self.block_rows), self.block_rows)

    def orientation(self, i, k):
        return self.orient_ref[k, i]


def add_up_scores(places, flips, row_ref, fwd_ref, u_ref, part_refs, store):
    count, fourier = u_ref.shape[0], u_ref.shape[1]
    picks, rows = places.picks, places.block_rows
    for i in range(count):
        products, row_parts = [], []
        for k in range(picks):
            j = places.orientation(i, k)
            for flip, part_ref in zip(flips, part_refs):
                where = places.rows(i, k, flip)
                real_u = u_ref[i, where, :fourier]
                imag_u = u_ref[i, where, fourier:]
                real_p = part_ref[j, :, :fourier].astype(jnp.float32)
                imag_p = part_ref[j, :, fourier:].astype(jnp.float32)
                products.append(
                    jnp.concatenate(
                        [
                            (real_p * real_u + imag_p * imag_u).astype(jnp.bfloat16),
                            (real_p * imag_u - imag_p * real_u).astype(jnp.bfloat16),
                        ],
                        axis=1,
                    )
                )
                row_parts.append(row_ref[where, :])
        by_row = jnp.dot(jnp.concatenate(products, axis=0), fwd_ref[...], preferred_element_type=jnp.float32)
        for k in range(picks):
            mixed = 0.0
            for s in range(len(flips)):
                at = k * len(flips) + s
                mixed = mixed + by_row[at * rows : (at + 1) * rows] * row_parts[at]
            store(k, i, jnp.sum(mixed, axis=0, keepdims=True))


def add_up_slices(places, flips, row_ref, back_ref, u_ref, rounded_ref, total):
    count, fourier = u_ref.shape[0], u_ref.shape[1]
    picks, rows = places.picks, places.block_rows
    total[...] = jnp.zeros_like(total)
    for i in range(count):
        mixed = []
        for k in range(picks):
            j = places.orientation(i, k)
            weight = rounded_ref[k, i : i + 1, :]
            for flip in flips:
                mixed.append((row_ref[places.rows(i, k, flip), :] * weight).astype(jnp.bfloat16))
        spread = jnp.dot(jnp.concatenate(mixed, axis=0), back_ref[...], preferred_element_type=jnp.float32)
        for k in range(picks):
            j = places.orientation(i, k)
            for s, flip in enumerate(flips):
                where = places.rows(i, k, flip)
                at = (k * len(flips) + s) * rows
                real_u = u_ref[i, where, :fourier]
                imag_u = u_ref[i, where, fourier:]
                real_e = spread[at : at + rows, :fourier]
                imag_e = spread[at : at + rows, fourier:]
                total[s, j, :, :fourier] += real_u * real_e - imag_u * imag_e
                total[s, j, :, fourier:] += real_u * imag_e + imag_u * real_e


def first_scores(me, block_index, orient, tables, u, parts, flips):
    count, fourier, width = u.shape
    picks = orient.shape[0]
    orient_count, slab_count = block_index.shape
    block_rows = parts[0].shape[1]

    def kernel(me_ref, index_ref, orient_ref, row_ref, fwd_ref, u_ref, *rest):
        part_refs, (score_ref, first_out, orient_out) = rest[:-3], rest[-3:]
        for j in range(orient_count):
            for flip in range(slab_count):
                first_out[j, flip] = index_ref[j, jnp.bitwise_xor(me_ref[0], flip)] * block_rows
        for i in range(count):
            for k in range(picks):
                orient_out[k, i] = orient_ref[k, i]
        places = Places(first_out, orient_out, block_rows)

        def store(k, i, value):
            score_ref[k, i : i + 1, :] = value

        add_up_scores(places, flips, row_ref, fwd_ref, u_ref, part_refs, store)

    return pl.pallas_call(
        kernel,
        out_shape=(
            pltpu.VMEM((picks, count, LANES), jnp.float32),
            pltpu.SMEM(block_index.shape, jnp.int32),
            pltpu.SMEM(orient.shape, jnp.int32),
        ),
        in_specs=[SMEM] * 3 + [VMEM] * (3 + len(parts)),
        out_specs=(VMEM, SMEM, SMEM),
        compiler_params=pltpu.CompilerParams(vmem_limit_bytes=VMEM_LIMIT),
        cost_estimate=pl.CostEstimate(
            flops=len(parts) * count * picks * block_rows * width * LANES * 2,
            bytes_accessed=4 * count * fourier * width,
            transcendentals=0,
        ),
        name="first_scores",
    )(me, block_index, orient, *tables[:2], u, *parts)


def expectation(first, orient, tables, u, parts, flips, scores, out_flips):
    count, fourier, width = u.shape
    picks = orient.shape[0]
    orient_count, block_rows, _ = parts[0].shape

    def kernel(first_ref, orient_ref, row_ref, fwd_ref, back_ref, u_ref, score_ref, *rest):
        part_refs = rest[: len(parts)]
        weights_ref, rounded_ref, rows_ref, total = rest[len(parts) :]
        places = Places(first_ref, orient_ref, block_rows)

        def store(k, i, value):
            rounded_ref[k, i : i + 1, :] = value

        add_up_scores(places, flips, row_ref, fwd_ref, u_ref, part_refs, store)
        squared = []
        for k in range(picks):
            value = rounded_ref[k] + score_ref[k]
            value = value + pltpu.roll(value, 2 * NS, 1)
            value = value + pltpu.roll(value, NS, 1)
            value = value * (1.0 / fourier)
            squared.append(value * value)
        mean = jnp.sum(sum(squared), axis=1, keepdims=True) * (1.0 / (LANES * picks))
        scale = 1.0 / (mean + 1e-05)
        lane = lax.broadcasted_iota(jnp.int32, (count, LANES), 1) // NS
        merged = jnp.zeros((count, LANES), jnp.float32)
        for k in range(picks):
            value = squared[k] * scale
            merged = jnp.where(lane == k, value, merged)
            rounded_ref[k] = value.astype(jnp.bfloat16).astype(jnp.float32)
        weights_ref[0] = merged[:, : picks * NS]
        add_up_slices(places, out_flips, row_ref, back_ref, u_ref, rounded_ref, total)
        rows_ref[...] = total[...].astype(jnp.bfloat16)

    return pl.pallas_call(
        kernel,
        out_shape=(
            pltpu.VMEM((1, count, picks * NS), jnp.float32),
            pltpu.VMEM((picks, count, LANES), jnp.float32),
            pltpu.VMEM((len(out_flips), orient_count, block_rows, width), jnp.bfloat16),
        ),
        in_specs=[SMEM] * 2 + [VMEM] * (5 + len(parts)),
        out_specs=(VMEM,) * 3,
        scratch_shapes=[pltpu.VMEM((len(out_flips), orient_count, block_rows, width), jnp.float32)],
        compiler_params=pltpu.CompilerParams(vmem_limit_bytes=VMEM_LIMIT),
        cost_estimate=pl.CostEstimate(
            flops=(len(parts) + len(out_flips)) * count * picks * block_rows * width * LANES * 2,
            bytes_accessed=4 * count * fourier * width,
            transcendentals=0,
        ),
        name="expectation",
    )(first, orient, *tables, u, scores, *parts)


def more_slices(first, orient, tables, u, rounded, block_rows, out_flips):
    count, fourier, width = u.shape
    picks, orient_count = orient.shape[0], first.shape[0]

    def kernel(first_ref, orient_ref, row_ref, back_ref, u_ref, rounded_ref, rows_ref, total):
        places = Places(first_ref, orient_ref, block_rows)
        add_up_slices(places, out_flips, row_ref, back_ref, u_ref, rounded_ref, total)
        rows_ref[...] = total[...].astype(jnp.bfloat16)

    return pl.pallas_call(
        kernel,
        out_shape=pltpu.VMEM((len(out_flips), orient_count, block_rows, width), jnp.bfloat16),
        in_specs=[SMEM] * 2 + [VMEM] * 4,
        out_specs=VMEM,
        scratch_shapes=[pltpu.VMEM((len(out_flips), orient_count, block_rows, width), jnp.float32)],
        compiler_params=pltpu.CompilerParams(vmem_limit_bytes=VMEM_LIMIT),
        cost_estimate=pl.CostEstimate(
            flops=len(out_flips) * count * picks * block_rows * width * LANES * 2,
            bytes_accessed=4 * count * fourier * width,
            transcendentals=0,
        ),
        name="more_slices",
    )(first, orient, tables[0], tables[2], u, rounded)


def swap(value, axis, size, flip):
    return lax.ppermute(value, axis, [(source, source ^ flip) for source in range(size)])


def together(*values):
    return sum(value.astype(jnp.float32) for value in values).astype(jnp.bfloat16)


def direct(volume, interp, block_index, images, defocus, orient):
    slab_count = lax.axis_size("slab")
    group_count = lax.axis_size("img")
    orient_count, block_rows, slab_rows = interp.shape[1:]
    fourier, width = images.shape[2:]
    image_count = images.shape[1] * slab_count
    near, far, other, side = 2, 4, 6, 1

    def to(value, flip):
        return swap(value, "slab", slab_count, flip)

    weigher = interp[0].reshape(orient_count * block_rows, slab_rows)
    own = jnp.dot(weigher, volume, preferred_element_type=jnp.float32).astype(jnp.bfloat16)
    own = own.reshape(orient_count, block_rows, width)
    from_other, from_far, from_near, from_side = (to(own, flip) for flip in (other, far, near, side))
    from_near_side = to(from_near, side)
    me = lax.axis_index("slab").astype(jnp.int32).reshape(1)
    u = weigh_images(images, defocus)
    from_far, from_other, u, from_side, from_near_side = lax.optimization_barrier((from_far, from_other, u, from_side, from_near_side))
    from_far_side, from_other_side = to(jnp.stack([from_far, from_other]), side)

    tables = separable_tables(fourier)
    scores, first, choice = first_scores(me, block_index[0], orient[0].T, tables, u, [own, from_near, from_far, from_other, from_side, from_near_side], (0, near, far, other, side, near + side))
    late_weigher, scores = lax.optimization_barrier((weigher, scores))
    weigher_across = swap(late_weigher, "img", group_count, 2)
    common = first, choice, tables, u
    weights, rounded, side_rows = expectation(
        *common,
        [from_far_side, from_other_side],
        (far + side, other + side),
        scores,
        (other + side,),
    )
    sent_first = to(side_rows[0], side)
    rest = to(more_slices(*common, rounded, block_rows, (far + side, near + side, side)), side)
    weigher_across, sent_first = lax.optimization_barrier((weigher_across, sent_first))
    rows = more_slices(*common, rounded, block_rows, (other, far, near, 0))
    back = together(
        rows[3],
        rest[2],
        to(together(rows[0], sent_first), other),
        to(together(rows[1], rest[0]), far),
        to(together(rows[2], rest[1]), near),
    ).reshape(orient_count * block_rows, width)

    def all_groups(value):
        across = swap(value, "img", group_count, 2)
        return [value, swap(value, "img", group_count, 1), across, swap(across, "img", group_count, 1)]

    weighers = [weigher, swap(weigher, "img", group_count, 1), weigher_across, swap(weigher_across, "img", group_count, 1)]
    backs = all_groups(back)
    update = lax.dot_general(
        jnp.concatenate(weighers, axis=0),
        jnp.concatenate(backs, axis=0),
        (((0,), (0,)), ((), ())),
        preferred_element_type=jnp.float32,
    )
    return update / math.sqrt(image_count), weights


def phase_tables(fourier, shifts, box):
    freq = (jnp.arange(fourier, dtype=jnp.int32) - fourier // 2).astype(jnp.float32)
    shift_steps = jnp.arange(shifts, dtype=jnp.int32)
    shift_x = (2 * (shift_steps // grid_side) - (grid_side - 1)).astype(jnp.float32)
    shift_y = (2 * (shift_steps % grid_side) - (grid_side - 1)).astype(jnp.float32)
    angle = 2.0 * math.pi / box * (freq[:, None, None] * shift_x + freq[None, :, None] * shift_y)
    forward = jnp.stack([jnp.cos(angle), jnp.sin(angle)], axis=1).reshape(
        2 * fourier * fourier, shifts
    )
    backward = jnp.stack([jnp.cos(angle), -jnp.sin(angle)], axis=1).reshape(
        2 * fourier * fourier, shifts
    )
    return (forward.astype(jnp.bfloat16), backward.T.astype(jnp.bfloat16))


def contrast(defocus_blk, fourier, box):
    freq = (jnp.arange(fourier, dtype=jnp.int32) - fourier // 2).astype(jnp.float32)
    wave_sq = (freq[:, None] * freq[:, None] + freq[None, :] * freq[None, :]) / (box * box)
    phase = math.pi * wave_length * defocus_blk[:, None, None] * wave_sq
    phase = phase - 0.5 * math.pi * aberration * wave_length**3 * wave_sq * wave_sq
    return -(math.sqrt(1.0 - amplitude * amplitude) * jnp.sin(phase) + amplitude * jnp.cos(phase))


def correlate(panels, image_blk, list_blk, defocus_blk, phase_fwd, phase_back, box):
    count = image_blk.shape[0]
    fourier = image_blk.shape[1]
    picks = list_blk.shape[1]
    shifts = phase_fwd.shape[1]
    ctf = contrast(defocus_blk, fourier, box)
    weighted = ctf[:, :, None, :] * image_blk.astype(jnp.float32).reshape(
        count, fourier, 2, fourier
    )
    real_u = weighted[:, None, :, 0]
    imag_u = weighted[:, None, :, 1]
    chosen = panels[list_blk].astype(jnp.float32).reshape(count, picks, fourier, 2, fourier)
    real_p = chosen[:, :, :, 0]
    imag_p = chosen[:, :, :, 1]
    product = jnp.stack(
        [real_p * real_u + imag_p * imag_u, real_p * imag_u - imag_p * real_u], axis=3
    )
    product = product.astype(jnp.bfloat16).reshape(count * picks, 2 * fourier * fourier)
    scores = jnp.dot(product, phase_fwd, preferred_element_type=jnp.float32) / fourier
    scores = scores.reshape(count, picks * shifts)
    squared = scores * scores
    weights = squared / (jnp.mean(squared, axis=1, keepdims=True) + 1e-05)
    rounded = weights.astype(jnp.bfloat16).reshape(count * picks, shifts)
    spread = jnp.dot(rounded, phase_back, preferred_element_type=jnp.float32)
    spread = spread.reshape(count, picks, fourier, 2, fourier)
    real_e = spread[:, :, :, 0]
    imag_e = spread[:, :, :, 1]
    backed = jnp.stack(
        [real_u * real_e - imag_u * imag_e, real_u * imag_e + imag_u * real_e], axis=3
    )
    backed = backed.astype(jnp.bfloat16).reshape(count * picks, 2 * fourier * fourier)
    return (weights, backed)


def through_owners(volume, interp, block_index, images, defocus, orient):
    slab_count = lax.axis_size("slab")
    slab_index = lax.axis_index("slab")
    orient_count = interp.shape[1]
    ori_dev = orient_count // slab_count
    block_rows = interp.shape[2]
    fourier = images.shape[2]
    block_count = fourier // block_rows
    img_dev = images.shape[1]
    picks = orient.shape[2]
    levels = jnp.arange(block_count, dtype=jnp.int32)
    partial_value = jnp.einsum("jpr,rx->jpx", interp[0], volume, preferred_element_type=jnp.float32)
    owned_idx = lax.dynamic_slice_in_dim(block_index[0], slab_index * ori_dev, ori_dev, 0)
    arrived = lax.all_to_all(partial_value, "slab", split_axis=0, concat_axis=0, tiled=True)
    arrived = arrived.reshape(slab_count, ori_dev, block_rows, 2 * fourier)
    chosen = (owned_idx[:, :, None] == levels).astype(jnp.float32)
    summed = jnp.einsum("osb,sopx->obpx", chosen, arrived, precision=lax.Precision.HIGHEST)
    summed = summed.reshape(ori_dev, fourier, 2 * fourier)
    panels = lax.all_gather(summed.astype(jnp.bfloat16), "slab", axis=0, tiled=True)
    phase_fwd, phase_back = phase_tables(fourier, NS, BOX)
    blk = math.gcd(img_dev, 32)
    blk_total = img_dev // blk

    def per_block(pieces):
        image_blk, list_blk, defocus_blk = pieces
        return correlate(panels, image_blk, list_blk, defocus_blk, phase_fwd, phase_back, BOX)

    weights, backs = lax.map(
        per_block,
        (
            images[0].reshape(blk_total, blk, fourier, 2 * fourier),
            orient[0].reshape(blk_total, blk, picks),
            defocus[0].reshape(blk_total, blk),
        ),
    )
    all_slices = backs.reshape(img_dev * picks, 2 * fourier * fourier)
    member = (
        orient[0].reshape(-1)[:, None] == jnp.arange(orient_count, dtype=jnp.int32)[None, :]
    ).astype(jnp.bfloat16)
    back_own = lax.psum_scatter(
        lax.dot_general(
            member, all_slices, (((0,), (0,)), ((), ())), preferred_element_type=jnp.float32
        ),
        "slab",
        scatter_dimension=0,
        tiled=True,
    ).astype(jnp.bfloat16)
    back_own = back_own.reshape(ori_dev, block_count, block_rows, 2 * fourier)
    chosen_back = (owned_idx[:, :, None] == levels).astype(jnp.bfloat16)
    outgoing = jnp.einsum(
        "osb,obpx->sopx", chosen_back, back_own, preferred_element_type=jnp.float32
    )
    outgoing = outgoing.astype(jnp.bfloat16).reshape(slab_count * ori_dev, block_rows, 2 * fourier)
    incoming = lax.all_to_all(outgoing, "slab", split_axis=0, concat_axis=0, tiled=True)
    column = jnp.einsum("jpr,jpx->rx", interp[0], incoming, preferred_element_type=jnp.float32)
    summed_cols = lax.psum(column, "img")
    update = summed_cols / math.sqrt(img_dev * slab_count)
    return (update, weights)


def on_device(volume, interp, block_index, images, defocus, orient):
    orient_count, block_rows = interp.shape[1:3]
    gathered = lax.axis_size("slab") * orient_count * block_rows * images.shape[3] * 2
    pairs = lax.axis_size("slab") == 8 and lax.axis_size("img") == 4
    plan = direct if pairs and gathered <= DIRECT_BYTES else through_owners
    return plan(volume, interp, block_index, images, defocus, orient)


def solution(mesh):
    return jax.shard_map(
        on_device,
        mesh=mesh,
        in_specs=(
            P("slab", None),
            P("img", None, None, "slab"),
            P("img", None, None),
            P("img", "slab", None, None),
            P("img", "slab"),
            P("img", "slab", None),
        ),
        out_specs=(P("slab", None), P("img", "slab", None)),
        check_vma=False,
    )
```

```python
import math

import jax
import jax.numpy as jnp
import numpy as np
from jax import lax
from jax.experimental import pallas as pl
from jax.experimental.pallas import tpu as pltpu
from jax.sharding import PartitionSpec as P

BOX = 256
NS = 16

wave_length = 0.0197
aberration = 27000000.0
amplitude = 0.1
grid_side = 4
LANES = 128
IMAGE_MOVES = 4
VMEM_LIMIT = 32 << 20
SMEM = pl.BlockSpec(memory_space=pltpu.SMEM)
VMEM = pl.BlockSpec(memory_space=pltpu.VMEM)
DIRECT_BYTES = 4 << 20


def split_bf16(values):
    high = values.astype(jnp.bfloat16)
    low = (values - high.astype(np.float64)).astype(jnp.bfloat16)
    return high, low


def separable_tables(fourier):
    freq = np.arange(fourier) - fourier // 2
    shift = np.arange(NS)
    shift_x = 2 * (shift // grid_side) - (grid_side - 1)
    shift_y = 2 * (shift % grid_side) - (grid_side - 1)
    row = 2.0 * math.pi / BOX * freq[:, None] * shift_x
    col = 2.0 * math.pi / BOX * freq[:, None] * shift_y
    row_table = np.concatenate([np.cos(row), np.sin(row)] * 4, axis=1).astype(np.float32)
    even = np.concatenate([np.cos(col), np.sin(col)], axis=0)
    odd = np.concatenate([-np.sin(col), np.cos(col)], axis=0)
    even_high, even_low = split_bf16(even)
    odd_high, odd_low = split_bf16(odd)
    col_fwd = np.concatenate([even_high, odd_high, even_low, odd_low] * 2, axis=1)
    even = np.concatenate([np.cos(col), -np.sin(col)], axis=0).T
    odd = np.concatenate([-np.sin(col), -np.cos(col)], axis=0).T
    even_high, even_low = split_bf16(even)
    odd_high, odd_low = split_bf16(odd)
    blank = np.zeros((LANES - 4 * NS, 2 * fourier), jnp.bfloat16)
    col_back = np.concatenate([even_high, odd_high, even_low, odd_low, blank], axis=0)
    return row_table, col_fwd, col_back


def sin_turns(turns):
    part = turns - jnp.round(turns)
    folded = jnp.where(part > 0.25, 0.5 - part, jnp.where(part < -0.25, -0.5 - part, part))
    x = folded * (2.0 * math.pi)
    y = x * x
    poly = -1.0 / 39916800.0
    for coefficient in (1.0 / 362880.0, -1.0 / 5040.0, 1.0 / 120.0, -1.0 / 6.0, 1.0):
        poly = poly * y + coefficient
    return x * poly


def weigh_images(images, defocus):
    _, count, fourier, width = images.shape

    def kernel(defocus_hbm, image_hbm, u_ref, defocus_ref, image_ref, defocus_sem, image_sems):
        moves = [pltpu.make_async_copy(defocus_hbm, defocus_ref, defocus_sem)]
        for part in range(IMAGE_MOVES):
            some = pl.ds(part * (count // IMAGE_MOVES), count // IMAGE_MOVES)
            moves.append(pltpu.make_async_copy(image_hbm.at[0, some], image_ref.at[some], image_sems.at[part]))
        for move in moves:
            move.start()
        kx = lax.broadcasted_iota(jnp.int32, (fourier, fourier), 0) - fourier // 2
        ky = lax.broadcasted_iota(jnp.int32, (fourier, fourier), 1) - fourier // 2
        wave_sq = (kx * kx + ky * ky).astype(jnp.float32) * (1.0 / (BOX * BOX))
        slope = wave_sq * (0.5 * wave_length)
        offset = wave_sq * wave_sq * (-0.25 * aberration * wave_length**3)
        offset = offset + math.asin(amplitude) / (2.0 * math.pi)
        moves[0].wait()
        for i in range(count):
            if i % (count // IMAGE_MOVES) == 0:
                moves[1 + i // (count // IMAGE_MOVES)].wait()
            ctf = -sin_turns(defocus_ref[0, i] * slope + offset)
            u_ref[i, :, :fourier] = ctf * image_ref[i, :, :fourier].astype(jnp.float32)
            u_ref[i, :, fourier:] = ctf * image_ref[i, :, fourier:].astype(jnp.float32)

    return pl.pallas_call(
        kernel,
        out_shape=pltpu.VMEM(images.shape[1:], jnp.float32),
        in_specs=[pl.BlockSpec(memory_space=pltpu.HBM)] * 2,
        out_specs=VMEM,
        scratch_shapes=[
            pltpu.SMEM(defocus.shape, defocus.dtype),
            pltpu.VMEM(images.shape[1:], images.dtype),
            pltpu.SemaphoreType.DMA,
            pltpu.SemaphoreType.DMA((IMAGE_MOVES,)),
        ],
        compiler_params=pltpu.CompilerParams(vmem_limit_bytes=VMEM_LIMIT),
        cost_estimate=pl.CostEstimate(
            flops=30 * count * fourier * fourier, bytes_accessed=6 * count * fourier * width, transcendentals=0
        ),
        name="weigh_images",
    )(*(pltpu.with_memory_space_constraint(value, pltpu.HBM) for value in (defocus, images)))


class Places:
    def __init__(self, first_ref, orient_ref, block_rows):
        self.first_ref, self.orient_ref, self.block_rows = first_ref, orient_ref, block_rows
        self.picks = orient_ref.shape[0]

    def rows(self, i, k, flip):
        first = self.first_ref[self.orient_ref[k, i], flip]
        return pl.ds(pl.multiple_of(first, self.block_rows), self.block_rows)

    def orientation(self, i, k):
        return self.orient_ref[k, i]


def add_up_scores(places, flips, row_ref, fwd_ref, u_ref, part_refs, store):
    count, fourier = u_ref.shape[0], u_ref.shape[1]
    picks, rows = places.picks, places.block_rows
    for i in range(count):
        products, row_parts = [], []
        for k in range(picks):
            j = places.orientation(i, k)
            for flip, part_ref in zip(flips, part_refs):
                where = places.rows(i, k, flip)
                real_u = u_ref[i, where, :fourier]
                imag_u = u_ref[i, where, fourier:]
                real_p = part_ref[j, :, :fourier].astype(jnp.float32)
                imag_p = part_ref[j, :, fourier:].astype(jnp.float32)
                products.append(
                    jnp.concatenate(
                        [
                            (real_p * real_u + imag_p * imag_u).astype(jnp.bfloat16),
                            (real_p * imag_u - imag_p * real_u).astype(jnp.bfloat16),
                        ],
                        axis=1,
                    )
                )
                row_parts.append(row_ref[where, :])
        by_row = jnp.dot(jnp.concatenate(products, axis=0), fwd_ref[...], preferred_element_type=jnp.float32)
        for k in range(picks):
            mixed = 0.0
            for s in range(len(flips)):
                at = k * len(flips) + s
                mixed = mixed + by_row[at * rows : (at + 1) * rows] * row_parts[at]
            store(k, i, jnp.sum(mixed, axis=0, keepdims=True))


def add_up_slices(places, flips, row_ref, back_ref, u_ref, rounded_ref, total):
    count, fourier = u_ref.shape[0], u_ref.shape[1]
    picks, rows = places.picks, places.block_rows
    total[...] = jnp.zeros_like(total)
    for i in range(count):
        mixed = []
        for k in range(picks):
            j = places.orientation(i, k)
            weight = rounded_ref[k, i : i + 1, :]
            for flip in flips:
                mixed.append((row_ref[places.rows(i, k, flip), :] * weight).astype(jnp.bfloat16))
        spread = jnp.dot(jnp.concatenate(mixed, axis=0), back_ref[...], preferred_element_type=jnp.float32)
        for k in range(picks):
            j = places.orientation(i, k)
            for s, flip in enumerate(flips):
                where = places.rows(i, k, flip)
                at = (k * len(flips) + s) * rows
                real_u = u_ref[i, where, :fourier]
                imag_u = u_ref[i, where, fourier:]
                real_e = spread[at : at + rows, :fourier]
                imag_e = spread[at : at + rows, fourier:]
                total[s, j, :, :fourier] += real_u * real_e - imag_u * imag_e
                total[s, j, :, fourier:] += real_u * imag_e + imag_u * real_e


def first_scores(me, block_index, orient, tables, u, parts, flips):
    count, fourier, width = u.shape
    picks = orient.shape[0]
    orient_count, slab_count = block_index.shape
    block_rows = parts[0].shape[1]

    def kernel(me_ref, index_ref, orient_ref, row_ref, fwd_ref, u_ref, *rest):
        part_refs, (score_ref, first_out, orient_out) = rest[:-3], rest[-3:]
        for j in range(orient_count):
            for flip in range(slab_count):
                first_out[j, flip] = index_ref[j, jnp.bitwise_xor(me_ref[0], flip)] * block_rows
        for i in range(count):
            for k in range(picks):
                orient_out[k, i] = orient_ref[k, i]
        places = Places(first_out, orient_out, block_rows)

        def store(k, i, value):
            score_ref[k, i : i + 1, :] = value

        add_up_scores(places, flips, row_ref, fwd_ref, u_ref, part_refs, store)

    return pl.pallas_call(
        kernel,
        out_shape=(
            pltpu.VMEM((picks, count, LANES), jnp.float32),
            pltpu.SMEM(block_index.shape, jnp.int32),
            pltpu.SMEM(orient.shape, jnp.int32),
        ),
        in_specs=[SMEM] * 3 + [VMEM] * (3 + len(parts)),
        out_specs=(VMEM, SMEM, SMEM),
        compiler_params=pltpu.CompilerParams(vmem_limit_bytes=VMEM_LIMIT),
        cost_estimate=pl.CostEstimate(
            flops=len(parts) * count * picks * block_rows * width * LANES * 2,
            bytes_accessed=4 * count * fourier * width,
            transcendentals=0,
        ),
        name="first_scores",
    )(me, block_index, orient, *tables[:2], u, *parts)


def more_scores(first, orient, tables, u, parts, flips, scores):
    count, fourier, width = u.shape
    picks = orient.shape[0]
    block_rows = parts[0].shape[1]

    def kernel(first_ref, orient_ref, row_ref, fwd_ref, u_ref, old_ref, *rest):
        part_refs, score_ref = rest[:-1], rest[-1]
        places = Places(first_ref, orient_ref, block_rows)

        def store(k, i, value):
            score_ref[k, i : i + 1, :] = value + old_ref[k, i : i + 1, :]

        add_up_scores(places, flips, row_ref, fwd_ref, u_ref, part_refs, store)

    return pl.pallas_call(
        kernel,
        out_shape=pltpu.VMEM((picks, count, LANES), jnp.float32),
        in_specs=[SMEM] * 2 + [VMEM] * (4 + len(parts)),
        out_specs=VMEM,
        compiler_params=pltpu.CompilerParams(vmem_limit_bytes=VMEM_LIMIT),
        cost_estimate=pl.CostEstimate(
            flops=len(parts) * count * picks * block_rows * width * LANES * 2,
            bytes_accessed=4 * count * fourier * width,
            transcendentals=0,
        ),
        name="more_scores",
    )(first, orient, *tables[:2], u, scores, *parts)


def expectation(first, orient, tables, u, parts, flips, scores, out_flips):
    count, fourier, width = u.shape
    picks = orient.shape[0]
    orient_count, block_rows, _ = parts[0].shape

    def kernel(first_ref, orient_ref, row_ref, fwd_ref, back_ref, u_ref, score_ref, *rest):
        part_refs = rest[: len(parts)]
        weights_ref, rounded_ref, rows_ref, total = rest[len(parts) :]
        places = Places(first_ref, orient_ref, block_rows)

        def store(k, i, value):
            rounded_ref[k, i : i + 1, :] = value

        add_up_scores(places, flips, row_ref, fwd_ref, u_ref, part_refs, store)
        squared = []
        for k in range(picks):
            value = rounded_ref[k] + score_ref[k]
            value = value + pltpu.roll(value, 2 * NS, 1)
            value = value + pltpu.roll(value, NS, 1)
            value = value * (1.0 / fourier)
            squared.append(value * value)
        mean = jnp.sum(sum(squared), axis=1, keepdims=True) * (1.0 / (LANES * picks))
        scale = 1.0 / (mean + 1e-05)
        lane = lax.broadcasted_iota(jnp.int32, (count, LANES), 1) // NS
        merged = jnp.zeros((count, LANES), jnp.float32)
        for k in range(picks):
            value = squared[k] * scale
            merged = jnp.where(lane == k, value, merged)
            rounded_ref[k] = value.astype(jnp.bfloat16).astype(jnp.float32)
        weights_ref[0] = merged[:, : picks * NS]
        add_up_slices(places, out_flips, row_ref, back_ref, u_ref, rounded_ref, total)
        rows_ref[...] = total[...].astype(jnp.bfloat16)

    return pl.pallas_call(
        kernel,
        out_shape=(
            pltpu.VMEM((1, count, picks * NS), jnp.float32),
            pltpu.VMEM((picks, count, LANES), jnp.float32),
            pltpu.VMEM((len(out_flips), orient_count, block_rows, width), jnp.bfloat16),
        ),
        in_specs=[SMEM] * 2 + [VMEM] * (5 + len(parts)),
        out_specs=(VMEM,) * 3,
        scratch_shapes=[pltpu.VMEM((len(out_flips), orient_count, block_rows, width), jnp.float32)],
        compiler_params=pltpu.CompilerParams(vmem_limit_bytes=VMEM_LIMIT),
        cost_estimate=pl.CostEstimate(
            flops=(len(parts) + len(out_flips)) * count * picks * block_rows * width * LANES * 2,
            bytes_accessed=4 * count * fourier * width,
            transcendentals=0,
        ),
        name="expectation",
    )(first, orient, *tables, u, scores, *parts)


def more_slices(first, orient, tables, u, rounded, block_rows, out_flips):
    count, fourier, width = u.shape
    picks, orient_count = orient.shape[0], first.shape[0]

    def kernel(first_ref, orient_ref, row_ref, back_ref, u_ref, rounded_ref, rows_ref, total):
        places = Places(first_ref, orient_ref, block_rows)
        add_up_slices(places, out_flips, row_ref, back_ref, u_ref, rounded_ref, total)
        rows_ref[...] = total[...].astype(jnp.bfloat16)

    return pl.pallas_call(
        kernel,
        out_shape=pltpu.VMEM((len(out_flips), orient_count, block_rows, width), jnp.bfloat16),
        in_specs=[SMEM] * 2 + [VMEM] * 4,
        out_specs=VMEM,
        scratch_shapes=[pltpu.VMEM((len(out_flips), orient_count, block_rows, width), jnp.float32)],
        compiler_params=pltpu.CompilerParams(vmem_limit_bytes=VMEM_LIMIT),
        cost_estimate=pl.CostEstimate(
            flops=len(out_flips) * count * picks * block_rows * width * LANES * 2,
            bytes_accessed=4 * count * fourier * width,
            transcendentals=0,
        ),
        name="more_slices",
    )(first, orient, tables[0], tables[2], u, rounded)


def swap(value, axis, size, flip):
    return lax.ppermute(value, axis, [(source, source ^ flip) for source in range(size)])


def together(*values):
    return sum(value.astype(jnp.float32) for value in values).astype(jnp.bfloat16)


def direct(volume, interp, block_index, images, defocus, orient):
    slab_count = lax.axis_size("slab")
    group_count = lax.axis_size("img")
    orient_count, block_rows, slab_rows = interp.shape[1:]
    fourier, width = images.shape[2:]
    image_count = images.shape[1] * slab_count
    near, far, other, side = 2, 4, 6, 1

    def to(value, flip):
        return swap(value, "slab", slab_count, flip)

    weigher = interp[0].reshape(orient_count * block_rows, slab_rows)
    own = jnp.dot(weigher, volume, preferred_element_type=jnp.float32).astype(jnp.bfloat16)
    own = own.reshape(orient_count, block_rows, width)
    from_near, from_far, from_other, from_side = (to(own, flip) for flip in (near, far, other, side))
    from_near_side = to(from_near, side)
    me = lax.axis_index("slab").astype(jnp.int32).reshape(1)
    u = weigh_images(images, defocus)
    from_far, u = lax.optimization_barrier((from_far, u))
    from_other, _ = lax.optimization_barrier((from_other, from_far))
    from_far_side, from_other_side = to(from_far, side), to(from_other, side)

    tables = separable_tables(fourier)
    scores, first, choice = first_scores(me, block_index[0], orient[0].T, tables, u, [own, from_near, from_far, from_other, from_side, from_near_side], (0, near, far, other, side, near + side))
    common = first, choice, tables, u
    scores = more_scores(*common, [from_far_side], (far + side,), scores)
    weights, rounded, side_rows = expectation(
        *common,
        [from_other_side],
        (other + side,),
        scores,
        (other + side,),
    )
    sent_first = to(side_rows[0], side)
    rest = to(more_slices(*common, rounded, block_rows, (far + side, near + side, side)), side)
    rows = more_slices(*common, rounded, block_rows, (other, far, near, 0))
    last = to(together(rows[0], sent_first), other)
    late_weigher, last = lax.optimization_barrier((weigher, last))
    back = together(
        rows[3],
        rest[2],
        last,
        to(together(rows[1], rest[0]), far),
        to(together(rows[2], rest[1]), near),
    ).reshape(orient_count * block_rows, width)

    def all_groups(value):
        across = swap(value, "img", group_count, 2)
        return [value, swap(value, "img", group_count, 1), across, swap(across, "img", group_count, 1)]

    weighers = all_groups(late_weigher)
    backs = all_groups(back)
    update = lax.dot_general(
        jnp.concatenate(weighers, axis=0),
        jnp.concatenate(backs, axis=0),
        (((0,), (0,)), ((), ())),
        preferred_element_type=jnp.float32,
    )
    return update / math.sqrt(image_count), weights


def phase_tables(fourier, shifts, box):
    freq = (jnp.arange(fourier, dtype=jnp.int32) - fourier // 2).astype(jnp.float32)
    shift_steps = jnp.arange(shifts, dtype=jnp.int32)
    shift_x = (2 * (shift_steps // grid_side) - (grid_side - 1)).astype(jnp.float32)
    shift_y = (2 * (shift_steps % grid_side) - (grid_side - 1)).astype(jnp.float32)
    angle = 2.0 * math.pi / box * (freq[:, None, None] * shift_x + freq[None, :, None] * shift_y)
    forward = jnp.stack([jnp.cos(angle), jnp.sin(angle)], axis=1).reshape(
        2 * fourier * fourier, shifts
    )
    backward = jnp.stack([jnp.cos(angle), -jnp.sin(angle)], axis=1).reshape(
        2 * fourier * fourier, shifts
    )
    return (forward.astype(jnp.bfloat16), backward.T.astype(jnp.bfloat16))


def contrast(defocus_blk, fourier, box):
    freq = (jnp.arange(fourier, dtype=jnp.int32) - fourier // 2).astype(jnp.float32)
    wave_sq = (freq[:, None] * freq[:, None] + freq[None, :] * freq[None, :]) / (box * box)
    phase = math.pi * wave_length * defocus_blk[:, None, None] * wave_sq
    phase = phase - 0.5 * math.pi * aberration * wave_length**3 * wave_sq * wave_sq
    return -(math.sqrt(1.0 - amplitude * amplitude) * jnp.sin(phase) + amplitude * jnp.cos(phase))


def correlate(panels, image_blk, list_blk, defocus_blk, phase_fwd, phase_back, box):
    count = image_blk.shape[0]
    fourier = image_blk.shape[1]
    picks = list_blk.shape[1]
    shifts = phase_fwd.shape[1]
    ctf = contrast(defocus_blk, fourier, box)
    weighted = ctf[:, :, None, :] * image_blk.astype(jnp.float32).reshape(
        count, fourier, 2, fourier
    )
    real_u = weighted[:, None, :, 0]
    imag_u = weighted[:, None, :, 1]
    chosen = panels[list_blk].astype(jnp.float32).reshape(count, picks, fourier, 2, fourier)
    real_p = chosen[:, :, :, 0]
    imag_p = chosen[:, :, :, 1]
    product = jnp.stack(
        [real_p * real_u + imag_p * imag_u, real_p * imag_u - imag_p * real_u], axis=3
    )
    product = product.astype(jnp.bfloat16).reshape(count * picks, 2 * fourier * fourier)
    scores = jnp.dot(product, phase_fwd, preferred_element_type=jnp.float32) / fourier
    scores = scores.reshape(count, picks * shifts)
    squared = scores * scores
    weights = squared / (jnp.mean(squared, axis=1, keepdims=True) + 1e-05)
    rounded = weights.astype(jnp.bfloat16).reshape(count * picks, shifts)
    spread = jnp.dot(rounded, phase_back, preferred_element_type=jnp.float32)
    spread = spread.reshape(count, picks, fourier, 2, fourier)
    real_e = spread[:, :, :, 0]
    imag_e = spread[:, :, :, 1]
    backed = jnp.stack(
        [real_u * real_e - imag_u * imag_e, real_u * imag_e + imag_u * real_e], axis=3
    )
    backed = backed.astype(jnp.bfloat16).reshape(count * picks, 2 * fourier * fourier)
    return (weights, backed)


def through_owners(volume, interp, block_index, images, defocus, orient):
    slab_count = lax.axis_size("slab")
    slab_index = lax.axis_index("slab")
    orient_count = interp.shape[1]
    ori_dev = orient_count // slab_count
    block_rows = interp.shape[2]
    fourier = images.shape[2]
    block_count = fourier // block_rows
    img_dev = images.shape[1]
    picks = orient.shape[2]
    levels = jnp.arange(block_count, dtype=jnp.int32)
    partial_value = jnp.einsum("jpr,rx->jpx", interp[0], volume, preferred_element_type=jnp.float32)
    owned_idx = lax.dynamic_slice_in_dim(block_index[0], slab_index * ori_dev, ori_dev, 0)
    arrived = lax.all_to_all(partial_value, "slab", split_axis=0, concat_axis=0, tiled=True)
    arrived = arrived.reshape(slab_count, ori_dev, block_rows, 2 * fourier)
    chosen = (owned_idx[:, :, None] == levels).astype(jnp.float32)
    summed = jnp.einsum("osb,sopx->obpx", chosen, arrived, precision=lax.Precision.HIGHEST)
    summed = summed.reshape(ori_dev, fourier, 2 * fourier)
    panels = lax.all_gather(summed.astype(jnp.bfloat16), "slab", axis=0, tiled=True)
    phase_fwd, phase_back = phase_tables(fourier, NS, BOX)
    blk = math.gcd(img_dev, 32)
    blk_total = img_dev // blk

    def per_block(pieces):
        image_blk, list_blk, defocus_blk = pieces
        return correlate(panels, image_blk, list_blk, defocus_blk, phase_fwd, phase_back, BOX)

    weights, backs = lax.map(
        per_block,
        (
            images[0].reshape(blk_total, blk, fourier, 2 * fourier),
            orient[0].reshape(blk_total, blk, picks),
            defocus[0].reshape(blk_total, blk),
        ),
    )
    all_slices = backs.reshape(img_dev * picks, 2 * fourier * fourier)
    member = (
        orient[0].reshape(-1)[:, None] == jnp.arange(orient_count, dtype=jnp.int32)[None, :]
    ).astype(jnp.bfloat16)
    back_own = lax.psum_scatter(
        lax.dot_general(
            member, all_slices, (((0,), (0,)), ((), ())), preferred_element_type=jnp.float32
        ),
        "slab",
        scatter_dimension=0,
        tiled=True,
    ).astype(jnp.bfloat16)
    back_own = back_own.reshape(ori_dev, block_count, block_rows, 2 * fourier)
    chosen_back = (owned_idx[:, :, None] == levels).astype(jnp.bfloat16)
    outgoing = jnp.einsum(
        "osb,obpx->sopx", chosen_back, back_own, preferred_element_type=jnp.float32
    )
    outgoing = outgoing.astype(jnp.bfloat16).reshape(slab_count * ori_dev, block_rows, 2 * fourier)
    incoming = lax.all_to_all(outgoing, "slab", split_axis=0, concat_axis=0, tiled=True)
    column = jnp.einsum("jpr,jpx->rx", interp[0], incoming, preferred_element_type=jnp.float32)
    summed_cols = lax.psum(column, "img")
    update = summed_cols / math.sqrt(img_dev * slab_count)
    return (update, weights)


def on_device(volume, interp, block_index, images, defocus, orient):
    orient_count, block_rows = interp.shape[1:3]
    gathered = lax.axis_size("slab") * orient_count * block_rows * images.shape[3] * 2
    pairs = lax.axis_size("slab") == 8 and lax.axis_size("img") == 4
    plan = direct if pairs and gathered <= DIRECT_BYTES else through_owners
    return plan(volume, interp, block_index, images, defocus, orient)


def solution(mesh):
    return jax.shard_map(
        on_device,
        mesh=mesh,
        in_specs=(
            P("slab", None),
            P("img", None, None, "slab"),
            P("img", None, None),
            P("img", "slab", None, None),
            P("img", "slab"),
            P("img", "slab", None),
        ),
        out_specs=(P("slab", None), P("img", "slab", None)),
        check_vma=False,
    )
```

```python
import math

import jax
import jax.numpy as jnp
import numpy as np
from jax import lax
from jax.experimental import pallas as pl
from jax.experimental.pallas import tpu as pltpu
from jax.sharding import PartitionSpec as P

BOX = 256
NS = 16

wave_length = 0.0197
aberration = 27000000.0
amplitude = 0.1
grid_side = 4
LANES = 128
IMAGE_MOVES = 4
VMEM_LIMIT = 32 << 20
SMEM = pl.BlockSpec(memory_space=pltpu.SMEM)
VMEM = pl.BlockSpec(memory_space=pltpu.VMEM)
DIRECT_BYTES = 4 << 20


def split_bf16(values):
    high = values.astype(jnp.bfloat16)
    low = (values - high.astype(np.float64)).astype(jnp.bfloat16)
    return high, low


def separable_tables(fourier):
    freq = np.arange(fourier) - fourier // 2
    shift = np.arange(NS)
    shift_x = 2 * (shift // grid_side) - (grid_side - 1)
    shift_y = 2 * (shift % grid_side) - (grid_side - 1)
    row = 2.0 * math.pi / BOX * freq[:, None] * shift_x
    col = 2.0 * math.pi / BOX * freq[:, None] * shift_y
    row_table = np.concatenate([np.cos(row), np.sin(row)] * 4, axis=1).astype(np.float32)
    even = np.concatenate([np.cos(col), np.sin(col)], axis=0)
    odd = np.concatenate([-np.sin(col), np.cos(col)], axis=0)
    even_high, even_low = split_bf16(even)
    odd_high, odd_low = split_bf16(odd)
    col_fwd = np.concatenate([even_high, odd_high, even_low, odd_low] * 2, axis=1)
    even = np.concatenate([np.cos(col), -np.sin(col)], axis=0).T
    odd = np.concatenate([-np.sin(col), -np.cos(col)], axis=0).T
    even_high, even_low = split_bf16(even)
    odd_high, odd_low = split_bf16(odd)
    blank = np.zeros((LANES - 4 * NS, 2 * fourier), jnp.bfloat16)
    col_back = np.concatenate([even_high, odd_high, even_low, odd_low, blank], axis=0)
    return row_table, col_fwd, col_back


def sin_turns(turns):
    part = turns - jnp.round(turns)
    folded = jnp.where(part > 0.25, 0.5 - part, jnp.where(part < -0.25, -0.5 - part, part))
    x = folded * (2.0 * math.pi)
    y = x * x
    poly = -1.0 / 39916800.0
    for coefficient in (1.0 / 362880.0, -1.0 / 5040.0, 1.0 / 120.0, -1.0 / 6.0, 1.0):
        poly = poly * y + coefficient
    return x * poly


def weigh_images(images, defocus):
    _, count, fourier, width = images.shape

    def kernel(defocus_hbm, image_hbm, u_ref, defocus_ref, image_ref, defocus_sem, image_sems):
        moves = [pltpu.make_async_copy(defocus_hbm, defocus_ref, defocus_sem)]
        for part in range(IMAGE_MOVES):
            some = pl.ds(part * (count // IMAGE_MOVES), count // IMAGE_MOVES)
            moves.append(pltpu.make_async_copy(image_hbm.at[0, some], image_ref.at[some], image_sems.at[part]))
        for move in moves:
            move.start()
        kx = lax.broadcasted_iota(jnp.int32, (fourier, fourier), 0) - fourier // 2
        ky = lax.broadcasted_iota(jnp.int32, (fourier, fourier), 1) - fourier // 2
        wave_sq = (kx * kx + ky * ky).astype(jnp.float32) * (1.0 / (BOX * BOX))
        slope = wave_sq * (0.5 * wave_length)
        offset = wave_sq * wave_sq * (-0.25 * aberration * wave_length**3)
        offset = offset + math.asin(amplitude) / (2.0 * math.pi)
        moves[0].wait()
        for i in range(count):
            if i % (count // IMAGE_MOVES) == 0:
                moves[1 + i // (count // IMAGE_MOVES)].wait()
            ctf = -sin_turns(defocus_ref[0, i] * slope + offset)
            u_ref[i, :, :fourier] = ctf * image_ref[i, :, :fourier].astype(jnp.float32)
            u_ref[i, :, fourier:] = ctf * image_ref[i, :, fourier:].astype(jnp.float32)

    return pl.pallas_call(
        kernel,
        out_shape=pltpu.VMEM(images.shape[1:], jnp.float32),
        in_specs=[pl.BlockSpec(memory_space=pltpu.HBM)] * 2,
        out_specs=VMEM,
        scratch_shapes=[
            pltpu.SMEM(defocus.shape, defocus.dtype),
            pltpu.VMEM(images.shape[1:], images.dtype),
            pltpu.SemaphoreType.DMA,
            pltpu.SemaphoreType.DMA((IMAGE_MOVES,)),
        ],
        compiler_params=pltpu.CompilerParams(vmem_limit_bytes=VMEM_LIMIT),
        cost_estimate=pl.CostEstimate(
            flops=30 * count * fourier * fourier, bytes_accessed=6 * count * fourier * width, transcendentals=0
        ),
        name="weigh_images",
    )(*(pltpu.with_memory_space_constraint(value, pltpu.HBM) for value in (defocus, images)))


class Places:
    def __init__(self, first_ref, orient_ref, block_rows):
        self.first_ref, self.orient_ref, self.block_rows = first_ref, orient_ref, block_rows
        self.picks = orient_ref.shape[0]

    def rows(self, i, k, flip):
        first = self.first_ref[self.orient_ref[k, i], flip]
        return pl.ds(pl.multiple_of(first, self.block_rows), self.block_rows)

    def orientation(self, i, k):
        return self.orient_ref[k, i]


def add_up_scores(places, flips, row_ref, fwd_ref, u_ref, part_refs, store):
    count, fourier = u_ref.shape[0], u_ref.shape[1]
    picks, rows = places.picks, places.block_rows
    for i in range(count):
        products, row_parts = [], []
        for k in range(picks):
            j = places.orientation(i, k)
            for flip, part_ref in zip(flips, part_refs):
                where = places.rows(i, k, flip)
                real_u = u_ref[i, where, :fourier]
                imag_u = u_ref[i, where, fourier:]
                real_p = part_ref[j, :, :fourier].astype(jnp.float32)
                imag_p = part_ref[j, :, fourier:].astype(jnp.float32)
                products.append(
                    jnp.concatenate(
                        [
                            (real_p * real_u + imag_p * imag_u).astype(jnp.bfloat16),
                            (real_p * imag_u - imag_p * real_u).astype(jnp.bfloat16),
                        ],
                        axis=1,
                    )
                )
                row_parts.append(row_ref[where, :])
        by_row = jnp.dot(jnp.concatenate(products, axis=0), fwd_ref[...], preferred_element_type=jnp.float32)
        for k in range(picks):
            mixed = 0.0
            for s in range(len(flips)):
                at = k * len(flips) + s
                mixed = mixed + by_row[at * rows : (at + 1) * rows] * row_parts[at]
            store(k, i, jnp.sum(mixed, axis=0, keepdims=True))


def add_up_slices(places, flips, row_ref, back_ref, u_ref, rounded_ref, total):
    count, fourier = u_ref.shape[0], u_ref.shape[1]
    picks, rows = places.picks, places.block_rows
    total[...] = jnp.zeros_like(total)
    for i in range(count):
        mixed = []
        for k in range(picks):
            j = places.orientation(i, k)
            weight = rounded_ref[k, i : i + 1, :]
            for flip in flips:
                mixed.append((row_ref[places.rows(i, k, flip), :] * weight).astype(jnp.bfloat16))
        spread = jnp.dot(jnp.concatenate(mixed, axis=0), back_ref[...], preferred_element_type=jnp.float32)
        for k in range(picks):
            j = places.orientation(i, k)
            for s, flip in enumerate(flips):
                where = places.rows(i, k, flip)
                at = (k * len(flips) + s) * rows
                real_u = u_ref[i, where, :fourier]
                imag_u = u_ref[i, where, fourier:]
                real_e = spread[at : at + rows, :fourier]
                imag_e = spread[at : at + rows, fourier:]
                total[s, j, :, :fourier] += real_u * real_e - imag_u * imag_e
                total[s, j, :, fourier:] += real_u * imag_e + imag_u * real_e


def first_scores(me, block_index, orient, tables, u, parts, flips):
    count, fourier, width = u.shape
    picks = orient.shape[0]
    orient_count, slab_count = block_index.shape
    block_rows = parts[0].shape[1]

    def kernel(me_ref, index_ref, orient_ref, row_ref, fwd_ref, u_ref, *rest):
        part_refs, (score_ref, first_out, orient_out) = rest[:-3], rest[-3:]
        for j in range(orient_count):
            for flip in range(slab_count):
                first_out[j, flip] = index_ref[j, jnp.bitwise_xor(me_ref[0], flip)] * block_rows
        for i in range(count):
            for k in range(picks):
                orient_out[k, i] = orient_ref[k, i]
        places = Places(first_out, orient_out, block_rows)

        def store(k, i, value):
            score_ref[k, i : i + 1, :] = value

        add_up_scores(places, flips, row_ref, fwd_ref, u_ref, part_refs, store)

    return pl.pallas_call(
        kernel,
        out_shape=(
            pltpu.VMEM((picks, count, LANES), jnp.float32),
            pltpu.SMEM(block_index.shape, jnp.int32),
            pltpu.SMEM(orient.shape, jnp.int32),
        ),
        in_specs=[SMEM] * 3 + [VMEM] * (3 + len(parts)),
        out_specs=(VMEM, SMEM, SMEM),
        compiler_params=pltpu.CompilerParams(vmem_limit_bytes=VMEM_LIMIT),
        cost_estimate=pl.CostEstimate(
            flops=len(parts) * count * picks * block_rows * width * LANES * 2,
            bytes_accessed=4 * count * fourier * width,
            transcendentals=0,
        ),
        name="first_scores",
    )(me, block_index, orient, *tables[:2], u, *parts)


def more_scores(first, orient, tables, u, parts, flips, scores):
    count, fourier, width = u.shape
    picks = orient.shape[0]
    block_rows = parts[0].shape[1]

    def kernel(first_ref, orient_ref, row_ref, fwd_ref, u_ref, old_ref, *rest):
        part_refs, score_ref = rest[:-1], rest[-1]
        places = Places(first_ref, orient_ref, block_rows)

        def store(k, i, value):
            score_ref[k, i : i + 1, :] = value + old_ref[k, i : i + 1, :]

        add_up_scores(places, flips, row_ref, fwd_ref, u_ref, part_refs, store)

    return pl.pallas_call(
        kernel,
        out_shape=pltpu.VMEM((picks, count, LANES), jnp.float32),
        in_specs=[SMEM] * 2 + [VMEM] * (4 + len(parts)),
        out_specs=VMEM,
        compiler_params=pltpu.CompilerParams(vmem_limit_bytes=VMEM_LIMIT),
        cost_estimate=pl.CostEstimate(
            flops=len(parts) * count * picks * block_rows * width * LANES * 2,
            bytes_accessed=4 * count * fourier * width,
            transcendentals=0,
        ),
        name="more_scores",
    )(first, orient, *tables[:2], u, scores, *parts)


def expectation(first, orient, tables, u, parts, flips, scores, out_flips):
    count, fourier, width = u.shape
    picks = orient.shape[0]
    orient_count, block_rows, _ = parts[0].shape

    def kernel(first_ref, orient_ref, row_ref, fwd_ref, back_ref, u_ref, score_ref, *rest):
        part_refs = rest[: len(parts)]
        weights_ref, rounded_ref, rows_ref, total = rest[len(parts) :]
        places = Places(first_ref, orient_ref, block_rows)

        def store(k, i, value):
            rounded_ref[k, i : i + 1, :] = value

        add_up_scores(places, flips, row_ref, fwd_ref, u_ref, part_refs, store)
        squared = []
        for k in range(picks):
            value = rounded_ref[k] + score_ref[k]
            value = value + pltpu.roll(value, 2 * NS, 1)
            value = value + pltpu.roll(value, NS, 1)
            value = value * (1.0 / fourier)
            squared.append(value * value)
        mean = jnp.sum(sum(squared), axis=1, keepdims=True) * (1.0 / (LANES * picks))
        scale = 1.0 / (mean + 1e-05)
        lane = lax.broadcasted_iota(jnp.int32, (count, LANES), 1) // NS
        merged = jnp.zeros((count, LANES), jnp.float32)
        for k in range(picks):
            value = squared[k] * scale
            merged = jnp.where(lane == k, value, merged)
            rounded_ref[k] = value.astype(jnp.bfloat16).astype(jnp.float32)
        weights_ref[0] = merged[:, : picks * NS]
        add_up_slices(places, out_flips, row_ref, back_ref, u_ref, rounded_ref, total)
        rows_ref[...] = total[...].astype(jnp.bfloat16)

    return pl.pallas_call(
        kernel,
        out_shape=(
            pltpu.VMEM((1, count, picks * NS), jnp.float32),
            pltpu.VMEM((picks, count, LANES), jnp.float32),
            pltpu.VMEM((len(out_flips), orient_count, block_rows, width), jnp.bfloat16),
        ),
        in_specs=[SMEM] * 2 + [VMEM] * (5 + len(parts)),
        out_specs=(VMEM,) * 3,
        scratch_shapes=[pltpu.VMEM((len(out_flips), orient_count, block_rows, width), jnp.float32)],
        compiler_params=pltpu.CompilerParams(vmem_limit_bytes=VMEM_LIMIT),
        cost_estimate=pl.CostEstimate(
            flops=(len(parts) + len(out_flips)) * count * picks * block_rows * width * LANES * 2,
            bytes_accessed=4 * count * fourier * width,
            transcendentals=0,
        ),
        name="expectation",
    )(first, orient, *tables, u, scores, *parts)


def more_slices(first, orient, tables, u, rounded, block_rows, out_flips):
    count, fourier, width = u.shape
    picks, orient_count = orient.shape[0], first.shape[0]

    def kernel(first_ref, orient_ref, row_ref, back_ref, u_ref, rounded_ref, rows_ref, total):
        places = Places(first_ref, orient_ref, block_rows)
        add_up_slices(places, out_flips, row_ref, back_ref, u_ref, rounded_ref, total)
        rows_ref[...] = total[...].astype(jnp.bfloat16)

    return pl.pallas_call(
        kernel,
        out_shape=pltpu.VMEM((len(out_flips), orient_count, block_rows, width), jnp.bfloat16),
        in_specs=[SMEM] * 2 + [VMEM] * 4,
        out_specs=VMEM,
        scratch_shapes=[pltpu.VMEM((len(out_flips), orient_count, block_rows, width), jnp.float32)],
        compiler_params=pltpu.CompilerParams(vmem_limit_bytes=VMEM_LIMIT),
        cost_estimate=pl.CostEstimate(
            flops=len(out_flips) * count * picks * block_rows * width * LANES * 2,
            bytes_accessed=4 * count * fourier * width,
            transcendentals=0,
        ),
        name="more_slices",
    )(first, orient, tables[0], tables[2], u, rounded)


def swap(value, axis, size, flip):
    return lax.ppermute(value, axis, [(source, source ^ flip) for source in range(size)])


def together(*values):
    return sum(value.astype(jnp.float32) for value in values).astype(jnp.bfloat16)


def direct(volume, interp, block_index, images, defocus, orient):
    slab_count = lax.axis_size("slab")
    group_count = lax.axis_size("img")
    orient_count, block_rows, slab_rows = interp.shape[1:]
    fourier, width = images.shape[2:]
    image_count = images.shape[1] * slab_count
    near, far, other, side = 2, 4, 6, 1

    def to(value, flip):
        return swap(value, "slab", slab_count, flip)

    weigher = interp[0].reshape(orient_count * block_rows, slab_rows)
    own = jnp.dot(weigher, volume, preferred_element_type=jnp.float32).astype(jnp.bfloat16)
    own = own.reshape(orient_count, block_rows, width)
    from_near, from_far, from_other, from_side = (to(own, flip) for flip in (near, far, other, side))
    from_near_side = to(from_near, side)
    me = lax.axis_index("slab").astype(jnp.int32).reshape(1)
    u = weigh_images(images, defocus)
    from_far, u = lax.optimization_barrier((from_far, u))
    from_other, _ = lax.optimization_barrier((from_other, from_far))
    from_far_side, from_other_side = to(from_far, side), to(from_other, side)

    tables = separable_tables(fourier)
    scores, first, choice = first_scores(me, block_index[0], orient[0].T, tables, u, [own, from_near, from_far, from_other, from_side, from_near_side], (0, near, far, other, side, near + side))
    common = first, choice, tables, u
    scores = more_scores(*common, [from_far_side], (far + side,), scores)
    weights, rounded, side_rows = expectation(
        *common,
        [from_other_side],
        (other + side,),
        scores,
        (other + side,),
    )
    sent_first = to(side_rows[0], side)
    rest = to(more_slices(*common, rounded, block_rows, (far + side, near + side, side)), side)
    rows = more_slices(*common, rounded, block_rows, (other, far, near, 0))
    last = to(together(rows[0], sent_first), other)
    late_weigher, rest = lax.optimization_barrier((weigher, rest))
    back = together(
        rows[3],
        rest[2],
        last,
        to(together(rows[1], rest[0]), far),
        to(together(rows[2], rest[1]), near),
    ).reshape(orient_count * block_rows, width)

    def all_groups(value):
        across = swap(value, "img", group_count, 2)
        return [value, swap(value, "img", group_count, 1), across, swap(across, "img", group_count, 1)]

    across = swap(late_weigher, "img", group_count, 2)
    weighers = [weigher, swap(weigher, "img", group_count, 1), across, swap(across, "img", group_count, 1)]
    backs = all_groups(back)
    def give_back(pair):
        return lax.dot_general(
            jnp.concatenate([weighers[i] for i in pair], axis=0),
            jnp.concatenate([backs[i] for i in pair], axis=0),
            (((0,), (0,)), ((), ())),
            preferred_element_type=jnp.float32,
        )

    update = lax.optimization_barrier(give_back((0, 2))) + give_back((1, 3))
    return update / math.sqrt(image_count), weights


def phase_tables(fourier, shifts, box):
    freq = (jnp.arange(fourier, dtype=jnp.int32) - fourier // 2).astype(jnp.float32)
    shift_steps = jnp.arange(shifts, dtype=jnp.int32)
    shift_x = (2 * (shift_steps // grid_side) - (grid_side - 1)).astype(jnp.float32)
    shift_y = (2 * (shift_steps % grid_side) - (grid_side - 1)).astype(jnp.float32)
    angle = 2.0 * math.pi / box * (freq[:, None, None] * shift_x + freq[None, :, None] * shift_y)
    forward = jnp.stack([jnp.cos(angle), jnp.sin(angle)], axis=1).reshape(
        2 * fourier * fourier, shifts
    )
    backward = jnp.stack([jnp.cos(angle), -jnp.sin(angle)], axis=1).reshape(
        2 * fourier * fourier, shifts
    )
    return (forward.astype(jnp.bfloat16), backward.T.astype(jnp.bfloat16))


def contrast(defocus_blk, fourier, box):
    freq = (jnp.arange(fourier, dtype=jnp.int32) - fourier // 2).astype(jnp.float32)
    wave_sq = (freq[:, None] * freq[:, None] + freq[None, :] * freq[None, :]) / (box * box)
    phase = math.pi * wave_length * defocus_blk[:, None, None] * wave_sq
    phase = phase - 0.5 * math.pi * aberration * wave_length**3 * wave_sq * wave_sq
    return -(math.sqrt(1.0 - amplitude * amplitude) * jnp.sin(phase) + amplitude * jnp.cos(phase))


def correlate(panels, image_blk, list_blk, defocus_blk, phase_fwd, phase_back, box):
    count = image_blk.shape[0]
    fourier = image_blk.shape[1]
    picks = list_blk.shape[1]
    shifts = phase_fwd.shape[1]
    ctf = contrast(defocus_blk, fourier, box)
    weighted = ctf[:, :, None, :] * image_blk.astype(jnp.float32).reshape(
        count, fourier, 2, fourier
    )
    real_u = weighted[:, None, :, 0]
    imag_u = weighted[:, None, :, 1]
    chosen = panels[list_blk].astype(jnp.float32).reshape(count, picks, fourier, 2, fourier)
    real_p = chosen[:, :, :, 0]
    imag_p = chosen[:, :, :, 1]
    product = jnp.stack(
        [real_p * real_u + imag_p * imag_u, real_p * imag_u - imag_p * real_u], axis=3
    )
    product = product.astype(jnp.bfloat16).reshape(count * picks, 2 * fourier * fourier)
    scores = jnp.dot(product, phase_fwd, preferred_element_type=jnp.float32) / fourier
    scores = scores.reshape(count, picks * shifts)
    squared = scores * scores
    weights = squared / (jnp.mean(squared, axis=1, keepdims=True) + 1e-05)
    rounded = weights.astype(jnp.bfloat16).reshape(count * picks, shifts)
    spread = jnp.dot(rounded, phase_back, preferred_element_type=jnp.float32)
    spread = spread.reshape(count, picks, fourier, 2, fourier)
    real_e = spread[:, :, :, 0]
    imag_e = spread[:, :, :, 1]
    backed = jnp.stack(
        [real_u * real_e - imag_u * imag_e, real_u * imag_e + imag_u * real_e], axis=3
    )
    backed = backed.astype(jnp.bfloat16).reshape(count * picks, 2 * fourier * fourier)
    return (weights, backed)


def through_owners(volume, interp, block_index, images, defocus, orient):
    slab_count = lax.axis_size("slab")
    slab_index = lax.axis_index("slab")
    orient_count = interp.shape[1]
    ori_dev = orient_count // slab_count
    block_rows = interp.shape[2]
    fourier = images.shape[2]
    block_count = fourier // block_rows
    img_dev = images.shape[1]
    picks = orient.shape[2]
    levels = jnp.arange(block_count, dtype=jnp.int32)
    partial_value = jnp.einsum("jpr,rx->jpx", interp[0], volume, preferred_element_type=jnp.float32)
    owned_idx = lax.dynamic_slice_in_dim(block_index[0], slab_index * ori_dev, ori_dev, 0)
    arrived = lax.all_to_all(partial_value, "slab", split_axis=0, concat_axis=0, tiled=True)
    arrived = arrived.reshape(slab_count, ori_dev, block_rows, 2 * fourier)
    chosen = (owned_idx[:, :, None] == levels).astype(jnp.float32)
    summed = jnp.einsum("osb,sopx->obpx", chosen, arrived, precision=lax.Precision.HIGHEST)
    summed = summed.reshape(ori_dev, fourier, 2 * fourier)
    panels = lax.all_gather(summed.astype(jnp.bfloat16), "slab", axis=0, tiled=True)
    phase_fwd, phase_back = phase_tables(fourier, NS, BOX)
    blk = math.gcd(img_dev, 32)
    blk_total = img_dev // blk

    def per_block(pieces):
        image_blk, list_blk, defocus_blk = pieces
        return correlate(panels, image_blk, list_blk, defocus_blk, phase_fwd, phase_back, BOX)

    weights, backs = lax.map(
        per_block,
        (
            images[0].reshape(blk_total, blk, fourier, 2 * fourier),
            orient[0].reshape(blk_total, blk, picks),
            defocus[0].reshape(blk_total, blk),
        ),
    )
    all_slices = backs.reshape(img_dev * picks, 2 * fourier * fourier)
    member = (
        orient[0].reshape(-1)[:, None] == jnp.arange(orient_count, dtype=jnp.int32)[None, :]
    ).astype(jnp.bfloat16)
    back_own = lax.psum_scatter(
        lax.dot_general(
            member, all_slices, (((0,), (0,)), ((), ())), preferred_element_type=jnp.float32
        ),
        "slab",
        scatter_dimension=0,
        tiled=True,
    ).astype(jnp.bfloat16)
    back_own = back_own.reshape(ori_dev, block_count, block_rows, 2 * fourier)
    chosen_back = (owned_idx[:, :, None] == levels).astype(jnp.bfloat16)
    outgoing = jnp.einsum(
        "osb,obpx->sopx", chosen_back, back_own, preferred_element_type=jnp.float32
    )
    outgoing = outgoing.astype(jnp.bfloat16).reshape(slab_count * ori_dev, block_rows, 2 * fourier)
    incoming = lax.all_to_all(outgoing, "slab", split_axis=0, concat_axis=0, tiled=True)
    column = jnp.einsum("jpr,jpx->rx", interp[0], incoming, preferred_element_type=jnp.float32)
    summed_cols = lax.psum(column, "img")
    update = summed_cols / math.sqrt(img_dev * slab_count)
    return (update, weights)


def on_device(volume, interp, block_index, images, defocus, orient):
    orient_count, block_rows = interp.shape[1:3]
    gathered = lax.axis_size("slab") * orient_count * block_rows * images.shape[3] * 2
    pairs = lax.axis_size("slab") == 8 and lax.axis_size("img") == 4
    plan = direct if pairs and gathered <= DIRECT_BYTES else through_owners
    return plan(volume, interp, block_index, images, defocus, orient)


def solution(mesh):
    return jax.shard_map(
        on_device,
        mesh=mesh,
        in_specs=(
            P("slab", None),
            P("img", None, None, "slab"),
            P("img", None, None),
            P("img", "slab", None, None),
            P("img", "slab"),
            P("img", "slab", None),
        ),
        out_specs=(P("slab", None), P("img", "slab", None)),
        check_vma=False,
    )
```
